256 devices in a mesh: dp: 2 (over core), seq: 32 (over z, y), head: 4 (over x).
Axes of the slice: x: 4, y: 4, z: 8, core: 2. Of those that a mesh axis runs over, the one named last changes fastest.
Arguments:
- prompt_key_input: bfloat16 [2, 6144, 512], P('dp', 'seq', 'head'), may hold values from -6 to 6
- prompt_value_input: bfloat16 [2, 6144, 512], P('dp', 'seq', 'head'), may hold values from -6 to 6
- resp_queries: bfloat16 [2, 32, 128, 4096], P('dp', 'seq', None, 'head'), may hold values from -6 to 6
- response_key_input: bfloat16 [2, 32, 128, 512], P('dp', 'seq', None, 'head'), may hold values from -6 to 6
- response_value_input: bfloat16 [2, 32, 128, 512], P('dp', 'seq', None, 'head'), may hold values from -6 to 6
- q_gain: float32 [128], replicated, may hold values from 0.5 to 3.5
- k_gain: float32 [128], replicated, may hold values from 0.5 to 3.5
- groups: int32 [2, 32], P('dp', 'seq'), may hold values from 0 to 1, as said below
- lengths: int32 [2, 32], P('dp', 'seq'), may hold values from 32 to 128, as said below
- tiles: int32 [2, 32, 48], P('dp', 'seq'), may hold values 0 or 1
- advantages: float32 [2, 32], P('dp', 'seq'), may hold values from -3 to 3
- upstream: bfloat16 [2, 32, 128, 4096], P('dp', 'seq', None, 'head'), may hold values from -6 to 6
Outputs:
- response_query_gradient: float32 [2, 32, 128, 4096], P('dp', 'seq', 'head')
- response_key_gradient: float32 [2, 32, 128, 512], P('dp', 'seq', None, 'head')
- grad_resp_values: float32 [2, 32, 128, 512], P('dp', 'seq', None, 'head')
- prompt_key_gradient: float32 [2, 6144, 512], P('dp', 'seq', 'head')
- prompt_value_gradient: float32 [2, 6144, 512], P('dp', 'seq', 'head')
- query_gain_gradient: float32 [128], replicated
- grad_k_gain: float32 [128], replicated
The draws below stay inside these ranges and needn't reach their ends.
Inputs may be any that keep to these rules, and one draw needn't show every extreme that they name: `groups`: each prompt 0 to 1 of a set is named by exactly 16 of its responses. `lengths`: in each set some response has length 128.
All inputs are finite; a program needn't handle non-finite values. No bound on the sum of `tiles` on one device may be relied on, other than what follows from the above.
Results may differ from the reference program's by a relative error of at most 0.008.
The reference program's roundings to bfloat16 on the way count: a program that leaves them out, or rounds other values in their place, can miss the bound.
Values may be sent and summed in bfloat16 or wider, within the bound.
No kernel may reach another device: no remote copies, remote signals or barrier semaphores. Data moves between devices by JAX's collectives and lax.ppermute only.
A program may use at most 128 MiB of HBM per device.

```python
import jax
import jax.numpy as jnp
from jax import lax

HEAD_WIDTH = 128
QUERY_PER_KEY = 8
KEY_HEADS = 4
QUERY_HEADS = 32
RESPONSE_TOKENS = 128
TILE = 64
SET_COUNT = 2
RESPONSE_COUNT = 32
GROUP = 16
PROMPT_COUNT = 2
PROMPT_TOKENS = 3072
TILES = 48


def response_base(key):
    return jnp.clip(jax.random.normal(key, (SET_COUNT, RESPONSE_COUNT, RESPONSE_TOKENS, KEY_HEADS * HEAD_WIDTH), jnp.float32), -6.0, 6.0)


def draw_response_key_input(key, part):
    initial_sample = response_base(key)
    return initial_sample.astype(jnp.bfloat16)


def draw_resp_queries(key, part):
    key = jax.random.fold_in(key, 5)
    queries = jnp.clip(jax.random.normal(key, (SET_COUNT, RESPONSE_COUNT, RESPONSE_TOKENS, QUERY_HEADS * HEAD_WIDTH), jnp.float32), -6.0, 6.0)
    return queries.astype(jnp.bfloat16)


def draw_q_gain(key, part):
    key = jax.random.fold_in(key, 7)
    return jax.random.uniform(key, (HEAD_WIDTH,), jnp.float32, 0.5, 1.5)


def draw_k_gain(key, part):
    key = jax.random.fold_in(key, 9)
    return jax.random.uniform(key, (HEAD_WIDTH,), jnp.float32, 0.5, 1.5)


def one_order(subkey):
    return jax.random.permutation(subkey, RESPONSE_COUNT)


def draw_groups(key, part):
    key = jax.random.fold_in(key, 11)
    subkeys = jax.random.split(key, SET_COUNT)
    orders = jax.vmap(one_order)(subkeys)
    return (orders // GROUP).astype(jnp.int32)


def draw_lengths(key, part):
    key = jax.random.fold_in(key, 13)
    first_key, second_key = jax.random.split(key)
    lowest = max(1, RESPONSE_TOKENS // 4)
    drawn = jax.random.randint(first_key, (SET_COUNT, RESPONSE_COUNT), lowest, RESPONSE_TOKENS + 1, dtype=jnp.int32)
    chosen = jax.random.randint(second_key, (SET_COUNT, 1), 0, RESPONSE_COUNT, dtype=jnp.int32)
    columns = jnp.arange(RESPONSE_COUNT, dtype=jnp.int32)[None, :]
    return jnp.where(columns == chosen, RESPONSE_TOKENS, drawn).astype(jnp.int32)


def with_ends(result, stream_key, least, high):
    index_at = [jax.random.randint(jax.random.fold_in(stream_key, axis), (), 0, length) for axis, length in enumerate(result.shape)]
    longest = result.shape.index(max(result.shape))
    next_to = index_at[:longest] + [(index_at[longest] + 1) % result.shape[longest]] + index_at[longest + 1:]
    return result.at[tuple(index_at)].set(least).at[tuple(next_to)].set(high)


def block_scale(rng, shape, pieces, low, largest):
    level = 1.0
    for axis_at, parts in pieces:
        draws = jax.random.uniform(jax.random.fold_in(jax.random.fold_in(rng, 6), axis_at), (parts,), jnp.float32, low / len(pieces), largest / len(pieces))
        level = level * jnp.repeat(jnp.exp(draws), shape[axis_at] // parts).reshape((-1,) + (1,) * (len(shape) - 1 - axis_at))
    return level


def gaussian(key, dims, spread, limit, shards=(), held_as=jnp.bfloat16):
    array = spread * jax.random.normal(key, dims, jnp.float32)
    if shards:
        array = array * block_scale(key, dims, shards, -0.22, 0.18)
    return jnp.clip(array, -limit, limit).astype(held_as)


def setup_inputs(seed: int = 0) -> dict:
    streams_of = jax.random.split(jax.random.key(seed), 13)
    prompt_key_input = gaussian(streams_of[0], (SET_COUNT, PROMPT_COUNT * PROMPT_TOKENS, KEY_HEADS * HEAD_WIDTH), 1.0, 6.0, ((0, 2), (1, 32), (2, 4)))
    prompt_value_input = gaussian(streams_of[1], (SET_COUNT, PROMPT_COUNT * PROMPT_TOKENS, KEY_HEADS * HEAD_WIDTH), 1.0, 6.0, ((0, 2), (1, 32), (2, 4)))
    resp_queries = draw_resp_queries(jax.random.fold_in(streams_of[12], 71), 0)
    response_key_input = draw_response_key_input(jax.random.fold_in(streams_of[12], 71), 0)
    response_value_input = gaussian(streams_of[4], (SET_COUNT, RESPONSE_COUNT, RESPONSE_TOKENS, KEY_HEADS * HEAD_WIDTH), 1.0, 6.0, ((0, 2), (1, 32), (3, 4)))
    q_gain = draw_q_gain(jax.random.fold_in(streams_of[12], 71), 0)
    k_gain = draw_k_gain(jax.random.fold_in(streams_of[12], 71), 0)
    groups = draw_groups(jax.random.fold_in(streams_of[12], 71), 0)
    lengths = draw_lengths(jax.random.fold_in(streams_of[12], 71), 0)
    tiles = with_ends((jax.random.randint(streams_of[9], (SET_COUNT, RESPONSE_COUNT, TILES), 0, 4) < 3).astype(jnp.int32), jax.random.fold_in(streams_of[9], 1), 0, 1)
    advantages = gaussian(streams_of[10], (SET_COUNT, RESPONSE_COUNT), 1.0, 3.0, ((0, 2), (1, 32)), jnp.float32)
    upstream = gaussian(streams_of[11], (SET_COUNT, RESPONSE_COUNT, RESPONSE_TOKENS, QUERY_HEADS * HEAD_WIDTH), 1.0, 6.0, ((0, 2), (1, 32), (3, 4)))
    return {"prompt_key_input": prompt_key_input, "prompt_value_input": prompt_value_input, "resp_queries": resp_queries, "response_key_input": response_key_input, "response_value_input": response_value_input, "q_gain": q_gain, "k_gain": k_gain, "groups": groups, "lengths": lengths, "tiles": tiles, "advantages": advantages, "upstream": upstream}


EPSILON = 1e-06
NEGATIVE = -1e+30

def head_norm(inputs, gains):
    return inputs * lax.rsqrt(lax.optimization_barrier(jnp.mean(inputs * inputs, axis=-1, keepdims=True)) + EPSILON) * gains

def matmul(left, right):
    return jnp.dot(left.astype(jnp.float32), right.astype(jnp.float32), preferred_element_type=jnp.float32)

def respond(query_rows, resp_key_rows, resp_val_rows, prompt_key_rows, prompt_val_rows, tile_row, resp_length, advantage, upstream_rows):
    score_scale = HEAD_WIDTH ** (-0.5)
    query_count = query_rows.shape[0]
    token_ids = jnp.arange(query_count, dtype=jnp.int32) // QUERY_PER_KEY
    prompt_allowed = (tile_row[jnp.arange(PROMPT_TOKENS, dtype=jnp.int32) // TILE] > 0)[None, :]
    resp_allowed = jnp.arange(RESPONSE_TOKENS, dtype=jnp.int32)[None, :] <= token_ids[:, None]
    prompt_scores = matmul(query_rows, prompt_key_rows.T) * score_scale
    resp_scores = matmul(query_rows, resp_key_rows.T) * score_scale
    row_max = jnp.maximum(lax.optimization_barrier(jnp.max(jnp.where(prompt_allowed, prompt_scores, NEGATIVE), axis=1)), lax.optimization_barrier(jnp.max(jnp.where(resp_allowed, resp_scores, NEGATIVE), axis=1)))
    row_sum = lax.optimization_barrier(jnp.sum(jnp.where(prompt_allowed, jnp.exp(prompt_scores - row_max[:, None]), 0.0), axis=1))
    row_sum = row_sum + lax.optimization_barrier(jnp.sum(jnp.where(resp_allowed, jnp.exp(resp_scores - row_max[:, None]), 0.0), axis=1))
    log_total = row_max + jnp.log(row_sum)
    prompt_probs = jnp.where(prompt_allowed, jnp.exp(prompt_scores - log_total[:, None]), 0.0)
    resp_probs = jnp.where(resp_allowed, jnp.exp(resp_scores - log_total[:, None]), 0.0)
    prompt_probs_b = prompt_probs.astype(jnp.bfloat16)
    resp_probs_b = resp_probs.astype(jnp.bfloat16)
    attended = matmul(prompt_probs_b, prompt_val_rows) + matmul(resp_probs_b, resp_val_rows)
    grad_out = jnp.where((token_ids < resp_length)[:, None], -advantage * upstream_rows.astype(jnp.float32), 0.0).astype(jnp.bfloat16)
    out_dot = lax.optimization_barrier(jnp.sum(grad_out.astype(jnp.float32) * attended, axis=1))
    grad_prompt_vals = matmul(prompt_probs_b.T, grad_out)
    grad_resp_vals = matmul(resp_probs_b.T, grad_out)
    prompt_grad_scores = (prompt_probs * (matmul(grad_out, prompt_val_rows.T) - out_dot[:, None])).astype(jnp.bfloat16)
    resp_grad_scores = (resp_probs * (matmul(grad_out, resp_val_rows.T) - out_dot[:, None])).astype(jnp.bfloat16)
    grad_query = (matmul(prompt_grad_scores, prompt_key_rows) + matmul(resp_grad_scores, resp_key_rows)) * score_scale
    prompt_key_gradient = matmul(prompt_grad_scores.T, query_rows) * score_scale
    response_key_gradient = matmul(resp_grad_scores.T, query_rows) * score_scale
    return (grad_query, response_key_gradient, grad_resp_vals, jnp.stack([prompt_key_gradient, grad_prompt_vals], axis=1))

def reference(prompt_key_input, prompt_value_input, resp_queries, response_key_input, response_value_input, q_gain, k_gain, groups, lengths, tiles, advantages, upstream):
    query_raw = resp_queries.astype(jnp.float32).reshape(SET_COUNT, RESPONSE_COUNT, RESPONSE_TOKENS, QUERY_HEADS, HEAD_WIDTH)
    query_full, query_back = jax.vjp(head_norm, query_raw, q_gain)
    query_hat = query_full.astype(jnp.bfloat16)
    unnormed_key = response_key_input.astype(jnp.float32).reshape(SET_COUNT, RESPONSE_COUNT, RESPONSE_TOKENS, KEY_HEADS, HEAD_WIDTH)
    key_full, key_back = jax.vjp(head_norm, unnormed_key, k_gain)
    key_hat = key_full.astype(jnp.bfloat16)
    response_value_rows = response_value_input.reshape(SET_COUNT, RESPONSE_COUNT, RESPONSE_TOKENS, KEY_HEADS, HEAD_WIDTH)
    unnormed_prompt = prompt_key_input.astype(jnp.float32).reshape(SET_COUNT, PROMPT_COUNT * PROMPT_TOKENS, KEY_HEADS, HEAD_WIDTH)
    prompt_full, prompt_back = jax.vjp(head_norm, unnormed_prompt, k_gain)
    prompt_hat = prompt_full.astype(jnp.bfloat16)
    prompt_value_rows = prompt_value_input.reshape(SET_COUNT, PROMPT_COUNT * PROMPT_TOKENS, KEY_HEADS, HEAD_WIDTH)
    upstream_heads = upstream.reshape(SET_COUNT, RESPONSE_COUNT, RESPONSE_TOKENS, QUERY_HEADS, HEAD_WIDTH)

    def visit_block(prompt_gradient_list, token_position):
        prompt_set_index = token_position // (RESPONSE_COUNT * KEY_HEADS)
        group_member = token_position // KEY_HEADS % RESPONSE_COUNT
        key_value_head = token_position % KEY_HEADS
        first_row = (groups[prompt_set_index, group_member] * PROMPT_TOKENS).astype(jnp.int32)
        query_rows = lax.dynamic_slice_in_dim(query_hat[prompt_set_index, group_member], key_value_head * QUERY_PER_KEY, QUERY_PER_KEY, 1).reshape(RESPONSE_TOKENS * QUERY_PER_KEY, HEAD_WIDTH)
        upstream_rows = lax.dynamic_slice_in_dim(upstream_heads[prompt_set_index, group_member], key_value_head * QUERY_PER_KEY, QUERY_PER_KEY, 1).reshape(RESPONSE_TOKENS * QUERY_PER_KEY, HEAD_WIDTH)
        prompt_key_rows = lax.dynamic_slice_in_dim(prompt_hat[prompt_set_index], first_row, PROMPT_TOKENS, 0)[:, key_value_head]
        prompt_val_rows = lax.dynamic_slice_in_dim(prompt_value_rows[prompt_set_index], first_row, PROMPT_TOKENS, 0)[:, key_value_head]
        grad_query, response_key_gradient, grad_resp_vals, grad_prompt = respond(query_rows, key_hat[prompt_set_index, group_member][:, key_value_head], response_value_rows[prompt_set_index, group_member][:, key_value_head], prompt_key_rows, prompt_val_rows, tiles[prompt_set_index, group_member], lengths[prompt_set_index, group_member], advantages[prompt_set_index, group_member], upstream_rows)
        root = jnp.zeros((), jnp.int32)
        corner = (prompt_set_index, first_row, key_value_head, root, root)
        current = lax.dynamic_slice(prompt_gradient_list, corner, (1, PROMPT_TOKENS, 1, 2, HEAD_WIDTH))
        prompt_gradient_list = lax.dynamic_update_slice(prompt_gradient_list, current + grad_prompt.reshape(1, PROMPT_TOKENS, 1, 2, HEAD_WIDTH), corner)
        return (prompt_gradient_list, (grad_query, response_key_gradient, grad_resp_vals))
    initial_gradients = jnp.zeros((SET_COUNT, PROMPT_COUNT * PROMPT_TOKENS, KEY_HEADS, 2, HEAD_WIDTH), jnp.float32)
    prompt_gradient_list, final_result = lax.scan(visit_block, initial_gradients, jnp.arange(SET_COUNT * RESPONSE_COUNT * KEY_HEADS, dtype=jnp.int32))
    query_gradient_total, key_gradient_total, value_gradient_total = final_result
    normed_query_gradient = query_gradient_total.reshape(SET_COUNT, RESPONSE_COUNT, KEY_HEADS, RESPONSE_TOKENS, QUERY_PER_KEY, HEAD_WIDTH).transpose(0, 1, 3, 2, 4, 5).reshape(SET_COUNT, RESPONSE_COUNT, RESPONSE_TOKENS, QUERY_HEADS, HEAD_WIDTH)
    normed_key_gradient = key_gradient_total.reshape(SET_COUNT, RESPONSE_COUNT, KEY_HEADS, RESPONSE_TOKENS, HEAD_WIDTH).transpose(0, 1, 3, 2, 4)
    value_gradient = value_gradient_total.reshape(SET_COUNT, RESPONSE_COUNT, KEY_HEADS, RESPONSE_TOKENS, HEAD_WIDTH).transpose(0, 1, 3, 2, 4)
    response_query_gradient, query_gain_gradient = query_back(normed_query_gradient)
    response_key_gradient, response_gain_factor = key_back(normed_key_gradient)
    prompt_key_gradient, prompt_gain_factor = prompt_back(prompt_gradient_list[:, :, :, 0])
    prompt_value_gradient = prompt_gradient_list[:, :, :, 1]
    return (response_query_gradient.reshape(SET_COUNT, RESPONSE_COUNT, RESPONSE_TOKENS, QUERY_HEADS * HEAD_WIDTH), response_key_gradient.reshape(SET_COUNT, RESPONSE_COUNT, RESPONSE_TOKENS, KEY_HEADS * HEAD_WIDTH), value_gradient.reshape(SET_COUNT, RESPONSE_COUNT, RESPONSE_TOKENS, KEY_HEADS * HEAD_WIDTH), prompt_key_gradient.reshape(SET_COUNT, PROMPT_COUNT * PROMPT_TOKENS, KEY_HEADS * HEAD_WIDTH), prompt_value_gradient.reshape(SET_COUNT, PROMPT_COUNT * PROMPT_TOKENS, KEY_HEADS * HEAD_WIDTH), query_gain_gradient, prompt_gain_factor + response_gain_factor)
```

```python
import functools

import jax
import jax.numpy as jnp
from jax import lax
from jax.experimental import pallas as pl
from jax.experimental.pallas import tpu as pltpu
from jax.sharding import Mesh
from jax.sharding import PartitionSpec as P

TILE = 64
HEAD = 128
HEADS = 8
TOKENS = 128
QUERIES = HEADS * TOKENS
ROWS = 192
Z = 8
Y = 4
X = 4
QUARTER = ROWS * Z // 2
CHUNK = 256
BLOCK = 256
PER_ROWS = ROWS // TILE
PER_PROMPT = PER_ROWS * Y
EPSILON = 1e-06
NEGATIVE = -1e30
SCALE = HEAD ** (-0.5)
SCALE2 = SCALE * 1.4426950408889634
VMEM = 56 * 1024 * 1024
F32 = jnp.float32
BF16 = jnp.bfloat16


def dot_nt(a, b):
    return lax.dot_general(a, b, (((1,), (1,)), ((), ())), preferred_element_type=F32)


def dot_nn(a, b):
    return jnp.dot(a, b, preferred_element_type=F32)


def dot_tn(a, b):
    return lax.dot_general(a, b, (((0,), (0,)), ((), ())), preferred_element_type=F32)


def unit(x):
    return x * lax.rsqrt(jnp.mean(x * x, axis=-1, keepdims=True) + EPSILON)


def norm_back(x, g, dy):
    r = lax.rsqrt(jnp.mean(x * x, axis=-1, keepdims=True) + EPSILON)
    u = x * r
    gy = g * dy
    return r * (gy - u * jnp.mean(u * gy, axis=-1, keepdims=True))


def responder(y, k):
    return lax.rem(y + (0, 1, 3, 2)[k], Y)


def responder_of(y, k):
    return lax.rem(y + jnp.where(k == 0, 0, jnp.where(k == 1, 1, jnp.where(k == 2, 3, 2))), Y)


def tile_bias(info, who, y, t):
    index = 1 + (t // PER_ROWS) * PER_PROMPT + y * PER_ROWS + t % PER_ROWS
    return jnp.where(info[who, index] > 0, 0.0, NEGATIVE).astype(F32)


def causal():
    v = lax.broadcasted_iota(jnp.int32, (TOKENS, TOKENS), 0)
    t = lax.broadcasted_iota(jnp.int32, (TOKENS, TOKENS), 1)
    return v <= t


def stats_kernel(pos, info, qg, kg, *refs):
    q = refs[:4]
    kv = refs[4:12]
    kr = refs[12]
    qh, kh, vh, ku, krh, out = refs[13:]
    y, z = pos[0], pos[1]
    for k in range(4):
        for j in range(HEADS):
            x = q[k][:, j * HEAD : (j + 1) * HEAD].astype(F32)
            qh[k, j * TOKENS : (j + 1) * TOKENS, :] = (unit(x) * qg[...]).astype(BF16)
    for s in range(Z):
        source = lax.rem(z + Z - (0, 1, 2, 3, 4, -1, -2, -3)[s], Z)
        rows = pl.ds(pl.multiple_of(source * ROWS, ROWS), ROWS)
        u = unit(kv[s][:, :HEAD].astype(F32))
        ku[rows, :] = u
        kh[rows, :] = (u * kg[...]).astype(BF16)
        vh[rows, :] = kv[s][:, HEAD:]
    krh[...] = (unit(kr[...].astype(F32)) * kg[...]).astype(BF16)
    mask = causal()

    def block(i, carry):
        k = i // 4
        b = i % 4
        who = responder_of(y, k)
        first = info[who, 0] * QUARTER
        qb = qh[k, pl.ds(pl.multiple_of(b * BLOCK, BLOCK), BLOCK), :]
        maxes, sums = [], []
        for c in range(QUARTER // CHUNK):
            keys = kh[pl.ds(pl.multiple_of(first + c * CHUNK, CHUNK), CHUNK), :]
            s = dot_nt(keys, qb) * SCALE2
            tiles = [s[t * TILE : (t + 1) * TILE] for t in range(CHUNK // TILE)]
            bias = [tile_bias(info, who, y, c * (CHUNK // TILE) + t) for t in range(CHUNK // TILE)]
            top = functools.reduce(
                jnp.maximum,
                [jnp.max(a, axis=0, keepdims=True) + v for a, v in zip(tiles, bias)],
            )
            top = jnp.maximum(top, 0.1 * NEGATIVE)
            sums.append(
                sum(
                    jnp.sum(jnp.exp2(a - (top - v)), axis=0, keepdims=True)
                    for a, v in zip(tiles, bias)
                )
            )
            maxes.append(top)
        top = functools.reduce(jnp.maximum, maxes)
        total = sum(s * jnp.exp2(m - top) for m, s in zip(maxes, sums))
        for h in range(BLOCK // TOKENS):
            for copy in range(Y):
                out[copy, who, pl.ds(b * 2 + h, 1), :] = top[:, h * TOKENS : (h + 1) * TOKENS]
                out[copy, who, pl.ds(8 + b * 2 + h, 1), :] = total[:, h * TOKENS : (h + 1) * TOKENS]
        return carry

    lax.fori_loop(0, 16, block, 0)
    for j in range(HEADS):
        s = dot_nt(krh[...], qh[0, j * TOKENS : (j + 1) * TOKENS, :]) * SCALE2
        s = jnp.where(mask, s, NEGATIVE)
        own = jnp.max(s, axis=0, keepdims=True)
        before = out[0, y, j : j + 1, :]
        top = jnp.maximum(own, before)
        total = jnp.sum(jnp.exp2(s - top), axis=0, keepdims=True)
        total = total + out[0, y, 8 + j : 9 + j, :] * jnp.exp2(before - top)
        for copy in range(Y):
            out[copy, y, j : j + 1, :] = top
            out[copy, y, 8 + j : 9 + j, :] = total


def values_kernel(pos, info, st, qh, kh, vh, krh, vr, *refs):
    go = refs[:4]
    dv, dvr, lt, out, gh = refs[4:]
    y = pos[0]
    for k in range(4):
        for j in range(HEADS):
            gh[k, j * TOKENS : (j + 1) * TOKENS, :] = go[k][:, j * HEAD : (j + 1) * HEAD]
        who = responder(y, k)
        top = functools.reduce(jnp.maximum, [st[s, who, 0:8, :] for s in range(Y)])
        total = sum(st[s, who, 8:16, :] * jnp.exp2(st[s, who, 0:8, :] - top) for s in range(Y))
        lt[k, :, :] = top + jnp.log2(total)
    dv[...] = jnp.zeros_like(dv)

    def block(i, carry):
        k = i // 4
        b = i % 4
        who = responder_of(y, k)
        first = info[who, 0] * QUARTER
        span = pl.ds(pl.multiple_of(b * BLOCK, BLOCK), BLOCK)
        qb = qh[k, span, :]
        gb = gh[k, span, :]
        row = jnp.concatenate([lt[k, pl.ds(b * 2 + h, 1), :] for h in range(2)], axis=1)
        dots = jnp.zeros((1, BLOCK), F32)
        for c in range(QUARTER // CHUNK):
            rows = pl.ds(pl.multiple_of(first + c * CHUNK, CHUNK), CHUNK)
            s = dot_nt(kh[rows, :], qb) * SCALE2
            g = dot_nt(vh[rows, :], gb)
            parts = []
            for t in range(CHUNK // TILE):
                v = tile_bias(info, who, y, c * (CHUNK // TILE) + t)
                span_t = slice(t * TILE, (t + 1) * TILE)
                p = jnp.exp2(s[span_t] - (row - v)).astype(BF16)
                parts.append(p)
                dots = dots + jnp.sum(p.astype(F32) * g[span_t], axis=0, keepdims=True)
            dv[rows, :] += dot_nn(jnp.concatenate(parts, axis=0), gb)
        for h in range(BLOCK // TOKENS):
            for copy in range(Y):
                out[copy, who, pl.ds(b * 2 + h, 1), :] = dots[:, h * TOKENS : (h + 1) * TOKENS]
        return carry

    lax.fori_loop(0, 16, block, 0)
    mask = causal()
    own = jnp.zeros((TOKENS, HEAD), F32)
    for j in range(HEADS):
        span = slice(j * TOKENS, (j + 1) * TOKENS)
        s = dot_nt(krh[...], qh[0, span, :]) * SCALE2
        p = jnp.where(mask, jnp.exp2(s - lt[0, j : j + 1, :]), 0.0).astype(BF16)
        g = dot_nt(vr[...], gh[0, span, :])
        dots = out[0, y, j : j + 1, :] + jnp.sum(p.astype(F32) * g, axis=0, keepdims=True)
        for copy in range(Y):
            out[copy, y, j : j + 1, :] = dots
        own = own + dot_nn(p, gh[0, span, :])
    dvr[...] = own


def grads_kernel(pos, info, dd, lt, qh, kh, vh, ku, krh, vr, gh, dv, qg, kg, kr, *refs):
    q = refs[:4]
    dq = refs[4:8]
    dkv, dkr, gains, kt, dots = refs[8:]
    y = pos[0]
    for k in range(4):
        who = responder(y, k)
        dots[k, :, :] = sum(dd[s, who, :, :] for s in range(Y))
    for p in range(2):
        kt[p, :, :] = kh[p * QUARTER : (p + 1) * QUARTER, :].T
    dkv[:, :HEAD] = jnp.zeros((2 * QUARTER, HEAD), F32)
    dkv[:, HEAD:] = dv[...]
    gains[...] = jnp.zeros_like(gains)

    def block_of(k, b):
        who = responder(y, k)
        group = info[who, 0]
        first = group * QUARTER
        span = pl.ds(pl.multiple_of(b * BLOCK, BLOCK), BLOCK)
        qb = qh[k, span, :]
        gb = gh[k, span, :]
        row = jnp.concatenate([lt[k, pl.ds(b * 2 + h, 1), :] for h in range(2)], axis=1)
        dot_row = jnp.concatenate([dots[k, pl.ds(b * 2 + h, 1), :] for h in range(2)], axis=1)
        total = jnp.zeros((HEAD, BLOCK), F32)
        for c in range(QUARTER // CHUNK):
            rows = pl.ds(pl.multiple_of(first + c * CHUNK, CHUNK), CHUNK)
            s = dot_nt(kh[rows, :], qb) * SCALE2
            g = dot_nt(vh[rows, :], gb)
            parts = []
            for t in range(CHUNK // TILE):
                v = tile_bias(info, who, y, c * (CHUNK // TILE) + t)
                span_t = slice(t * TILE, (t + 1) * TILE)
                p = jnp.exp2(s[span_t] - (row - v))
                parts.append((p * (g[span_t] - dot_row)).astype(BF16))
            ds = jnp.concatenate(parts, axis=0)
            dkv[rows, :HEAD] += dot_nn(ds, qb)
            total = total + dot_nn(kt[group, :, c * CHUNK : (c + 1) * CHUNK], ds)
        total = total * SCALE
        for h in range(BLOCK // TOKENS):
            lanes = pl.ds(pl.multiple_of(b * BLOCK + h * HEAD, HEAD), HEAD)
            dq[k][:, lanes] = total[:, h * TOKENS : (h + 1) * TOKENS].T

    mask = causal()
    for k in (3, 1, 2, 0):
        lax.fori_loop(0, 4, lambda b, carry, k=k: (block_of(k, b), carry)[1], 0)
    own = jnp.zeros((TOKENS, HEAD), F32)
    for j in range(HEADS):
        span = slice(j * TOKENS, (j + 1) * TOKENS)
        qb = qh[0, span, :]
        s = dot_nt(krh[...], qb) * SCALE2
        p = jnp.where(mask, jnp.exp2(s - lt[0, j : j + 1, :]), 0.0)
        g = dot_nt(vr[...], gh[0, span, :])
        ds = (p * (g - dots[0, j : j + 1, :])).astype(BF16)
        own = own + dot_nn(ds, qb)
        dq[0][:, j * HEAD : (j + 1) * HEAD] += dot_tn(ds, krh[...]) * SCALE
    dkv[:, :HEAD] = dkv[:, :HEAD] * SCALE
    own = own * SCALE
    x = kr[...].astype(F32)
    dkr[...] = norm_back(x, kg[...], own)
    gain_k = jnp.sum(dkv[:, :HEAD] * ku[...], axis=0, keepdims=True)
    gain_k = gain_k + jnp.sum(own * unit(x), axis=0, keepdims=True)
    gain_q = jnp.zeros((1, HEAD), F32)
    for k in range(4):
        for j in range(HEADS):
            span = slice(j * HEAD, (j + 1) * HEAD)
            gain_q = gain_q + jnp.sum(
                dq[k][:, span] * unit(q[k][:, span].astype(F32)), axis=0, keepdims=True
            )
    gains[0:1, :] = gain_q
    gains[1:2, :] = gain_k


def query_back_kernel(q, qg, mine, left, right, out):
    for j in range(HEADS):
        span = slice(j * HEAD, (j + 1) * HEAD)
        dy = mine[:, span] + left[:, span] + right[:, span]
        out[:, span] = norm_back(q[:, span].astype(F32), qg[...], dy).astype(BF16)


def key_back_kernel(k, kg, mine, left, right, dk, dv):
    dy = mine[...] + left[...] + right[...]
    dk[...] = norm_back(k[...].astype(F32), kg[...], dy[:, :HEAD])
    dv[...] = dy[:, HEAD:]


def spread_kernel(parts, out):
    for h in range(X):
        out[:, h * QUERIES : (h + 1) * QUERIES] = parts[h].astype(F32)


def call(kernel, out_shape, n_scalar, args, scratch=(), flops=0, nbytes=0):
    specs = [pl.BlockSpec(memory_space=pltpu.SMEM)] * n_scalar
    specs += [pl.BlockSpec(memory_space=pltpu.VMEM)] * (len(args) - n_scalar)
    return pl.pallas_call(
        kernel,
        out_shape=out_shape,
        in_specs=specs,
        out_specs=jax.tree.map(lambda _: pl.BlockSpec(memory_space=pltpu.VMEM), out_shape),
        scratch_shapes=scratch,
        compiler_params=pltpu.CompilerParams(vmem_limit_bytes=VMEM),
        cost_estimate=pl.CostEstimate(flops=flops, bytes_accessed=nbytes, transcendentals=0),
    )(*args)


def f32(*shape):
    return jax.ShapeDtypeStruct(shape, F32)


def bf16(*shape):
    return jax.ShapeDtypeStruct(shape, BF16)


def shift(x, axis, size, step):
    return lax.ppermute(x, axis, [(i, (i + step) % size) for i in range(size)])


def to_all(x, axis):
    return lax.all_to_all(x, axis, 0, 0, tiled=False)


def shards(
    prompt_key_input,
    prompt_value_input,
    resp_queries,
    response_key_input,
    response_value_input,
    q_gain,
    k_gain,
    groups,
    lengths,
    tiles,
    advantages,
    upstream,
):
    y = lax.axis_index("y")
    z = lax.axis_index("z")
    pos = jnp.stack([y, z]).astype(jnp.int32)
    qg = q_gain[None]
    kg = k_gain[None]
    k_raw = prompt_key_input[0]
    q_raw = resp_queries[0, 0]
    kr = response_key_input[0, 0]
    vr = response_value_input[0, 0]
    info = jnp.concatenate([groups[0], tiles[0, 0], jnp.zeros((79,), jnp.int32)])
    info = to_all(jnp.broadcast_to(info[None], (Y, 128)), "y").reshape(Y, 128)

    kv = jnp.concatenate([k_raw, prompt_value_input[0]], axis=1)
    q_before = shift(q_raw, "y", Y, 1)
    q_next = shift(q_raw, "y", Y, -1)
    q_far = shift(q_before, "y", Y, 1)
    up = [kv]
    down = []
    for s in range(Z // 2):
        up.append(shift(up[-1], "z", Z, 1))
        if s < Z // 2 - 1:
            down.append(shift(down[-1] if down else kv, "z", Z, -1))
    tokens = jnp.arange(TOKENS, dtype=jnp.int32)[:, None]
    go = jnp.where(
        tokens < lengths[0, 0], -advantages[0, 0] * upstream[0, 0].astype(F32), 0.0
    ).astype(BF16)
    go_before = shift(go, "y", Y, 1)
    go_next = shift(go, "y", Y, -1)
    go_far = shift(go_next, "y", Y, -1)
    qs = (q_raw, q_next, q_before, q_far)
    gos = (go, go_next, go_before, go_far)

    unit_flops = 2 * 4 * QUERIES * QUARTER * HEAD
    qh, kh, vh, ku, krh, st = call(
        stats_kernel,
        (
            bf16(4, QUERIES, HEAD),
            bf16(2 * QUARTER, HEAD),
            bf16(2 * QUARTER, HEAD),
            f32(2 * QUARTER, HEAD),
            bf16(TOKENS, HEAD),
            f32(Y, Y, 16, 128),
        ),
        2,
        (pos, info, qg, kg, *qs, *up, *down, kr),
        flops=2 * unit_flops,
        nbytes=1 << 22,
    )
    st = to_all(st, "y")
    dv, dvr, lt, dd, gh = call(
        values_kernel,
        (
            f32(2 * QUARTER, HEAD),
            f32(TOKENS, HEAD),
            f32(4, HEADS, 128),
            f32(Y, Y, HEADS, 128),
            bf16(4, QUERIES, HEAD),
        ),
        2,
        (pos, info, st, qh, kh, vh, krh, vr, *gos),
        flops=4 * unit_flops,
        nbytes=1 << 22,
    )
    dd = to_all(dd, "y")
    dq0, dq1, dq2, dq3, dkv, dkr, gains = call(
        grads_kernel,
        (
            *[f32(TOKENS, QUERIES)] * 4,
            f32(2 * QUARTER, 2 * HEAD),
            f32(TOKENS, HEAD),
            f32(8, HEAD),
        ),
        2,
        (pos, info, dd, lt, qh, kh, vh, ku, krh, vr, gh, dv, qg, kg, kr, *qs),
        scratch=[
            pltpu.VMEM((2, HEAD, QUARTER), BF16),
            pltpu.VMEM((4, HEADS, 128), F32),
        ],
        flops=5 * unit_flops,
        nbytes=1 << 22,
    )

    half = QUERIES // 2
    far_up = shift(dq3[:, :half], "y", Y, 1)
    far_down = shift(dq3[:, half:], "y", Y, -1)
    to_next = jnp.concatenate([dq1[:, :half] + far_up, dq1[:, half:]], axis=1)
    to_before = jnp.concatenate([dq2[:, :half], dq2[:, half:] + far_down], axis=1)
    from_before = shift(to_next, "y", Y, 1)
    from_next = shift(to_before, "y", Y, -1)

    dkv = dkv.reshape(Z, ROWS, 2 * HEAD)

    def piece(step):
        return lax.dynamic_index_in_dim(dkv, lax.rem(z + step + Z, Z), 0, keepdims=False)

    rising = shift(piece(4), "z", Z, 1)
    falling = shift(piece(-3), "z", Z, -1)
    for s in (3, 2, 1):
        rising = shift(rising + piece(s), "z", Z, 1)
        if s > 1:
            falling = shift(falling + piece(1 - s), "z", Z, -1)

    dq = call(
        query_back_kernel,
        bf16(TOKENS, QUERIES),
        0,
        (q_raw, qg, dq0, from_before, from_next),
        nbytes=1 << 21,
    )
    dq = to_all(dq.reshape(X, TOKENS // X, QUERIES), "head")
    regrouped = call(spread_kernel, f32(TOKENS // X, X * QUERIES), 0, (dq,), nbytes=1 << 20)
    dk, dv = call(
        key_back_kernel,
        (f32(ROWS, HEAD), f32(ROWS, HEAD)),
        0,
        (k_raw, kg, piece(0), rising, falling),
        nbytes=1 << 20,
    )
    gains = gains[:2]
    gains = gains + lax.ppermute(gains, "dp", [(0, 1), (1, 0)])
    for axis, size in (("head", X), ("y", Y), ("z", Z)):
        gains = jnp.sum(to_all(jnp.broadcast_to(gains[None], (size, 2, HEAD)), axis), axis=0)
    return (
        regrouped[None, None],
        dkr[None, None],
        dvr[None, None],
        dk[None],
        dv[None],
        gains[0],
        gains[1],
    )


def solution(mesh):
    sizes = mesh.devices.shape
    split = Mesh(mesh.devices.reshape(sizes[0], Z, Y, sizes[2]), ("dp", "z", "y", "head"))
    seq = ("z", "y")
    placed = (
        P("dp", seq, "head"),
        P("dp", seq, "head"),
        P("dp", seq, None, "head"),
        P("dp", seq, None, "head"),
        P("dp", seq, None, "head"),
        P(),
        P(),
        P("dp", seq),
        P("dp", seq),
        P("dp", seq, None),
        P("dp", seq),
        P("dp", seq, None, "head"),
    )
    return jax.shard_map(
        shards,
        mesh=split,
        in_specs=placed,
        out_specs=(
            P("dp", seq, "head", None),
            P("dp", seq, None, "head"),
            P("dp", seq, None, "head"),
            P("dp", seq, "head"),
            P("dp", seq, "head"),
            P(),
            P(),
        ),
        check_vma=False,
    )
```

```python
import functools

import jax
import jax.numpy as jnp
from jax import lax
from jax.experimental import pallas as pl
from jax.experimental.pallas import tpu as pltpu
from jax.sharding import Mesh
from jax.sharding import PartitionSpec as P

TILE = 64
HEAD = 128
HEADS = 8
TOKENS = 128
QUERIES = HEADS * TOKENS
ROWS = 192
Z = 8
Y = 4
X = 4
QUARTER = ROWS * Z // 2
BLOCK = 256
PART = TOKENS // X
PER_ROWS = ROWS // TILE
PER_PROMPT = PER_ROWS * Y
EPSILON = 1e-06
NEGATIVE = -1e30
SCALE = HEAD ** (-0.5)
SCALE2 = SCALE * 1.4426950408889634
VMEM = 56 * 1024 * 1024
SMALL = 12 * 1024 * 1024
F32 = jnp.float32
BF16 = jnp.bfloat16


def dot_nt(a, b):
    return lax.dot_general(a, b, (((1,), (1,)), ((), ())), preferred_element_type=F32)


def dot_nn(a, b):
    return jnp.dot(a, b, preferred_element_type=F32)


def dot_tn(a, b):
    return lax.dot_general(a, b, (((0,), (0,)), ((), ())), preferred_element_type=F32)


def unit(x):
    return x * lax.rsqrt(jnp.mean(x * x, axis=-1, keepdims=True) + EPSILON)


def norm_back(x, g, dy):
    r = lax.rsqrt(jnp.mean(x * x, axis=-1, keepdims=True) + EPSILON)
    u = x * r
    gy = g * dy
    return r * (gy - u * jnp.mean(u * gy, axis=-1, keepdims=True))


def responder(y, k):
    return lax.rem(y + (0, 1, 3, 2)[k], Y)


def heads_of(ref, first, count):
    return jnp.concatenate(
        [ref[:, j * HEAD : (j + 1) * HEAD] for j in range(first, first + count)], axis=0
    )


def tile_bias(info, who, y, t):
    index = 1 + (t // PER_ROWS) * PER_PROMPT + y * PER_ROWS + t % PER_ROWS
    return jnp.where(info[who, index] > 0, 0.0, NEGATIVE).astype(F32)


def causal():
    v = lax.broadcasted_iota(jnp.int32, (TOKENS, QUERIES), 0)
    t = lax.broadcasted_iota(jnp.int32, (TOKENS, QUERIES), 1) % TOKENS
    return v <= t


def joined(ref, k, first, count):
    return jnp.concatenate([ref[k, h : h + 1, :] for h in range(first, first + count)], axis=1)


def tiles_of(x):
    return [x[t * TILE : (t + 1) * TILE] for t in range(QUARTER // TILE)]


def biases_of(info, who, y):
    return [tile_bias(info, who, y, t) for t in range(QUARTER // TILE)]


def stats_kernel(pos, info, qg, kg, *refs):
    q = refs[:4]
    kv = refs[4]
    kr = refs[5]
    qh, kh, krh, out = refs[6:]
    y = pos[0]
    kh[...] = (unit(kv[:, :HEAD].astype(F32)) * kg[...]).astype(BF16)
    krh[...] = (unit(kr[...].astype(F32)) * kg[...]).astype(BF16)
    for k in range(4):
        for j in range(HEADS):
            u = unit(q[k][:, j * HEAD : (j + 1) * HEAD].astype(F32))
            qh[k, j * TOKENS : (j + 1) * TOKENS, :] = (u * qg[...]).astype(BF16)
    own = jnp.where(causal(), dot_nt(krh[...], qh[0]) * SCALE2, NEGATIVE)
    own_top = jnp.max(own, axis=0, keepdims=True)
    own_sum = jnp.sum(jnp.exp2(own - own_top), axis=0, keepdims=True)
    for k in range(4):
        who = responder(y, k)
        first = pl.multiple_of(info[k, 0] * QUARTER, QUARTER)
        keys = kh[pl.ds(first, QUARTER), :]
        bias = biases_of(info, k, y)
        for b in range(QUERIES // BLOCK):
            qb = qh[k, b * BLOCK : (b + 1) * BLOCK, :]
            tiles = tiles_of(dot_nt(keys, qb) * SCALE2)
            top = functools.reduce(
                jnp.maximum,
                [jnp.max(a, axis=0, keepdims=True) + v for a, v in zip(tiles, bias)],
            )
            top = jnp.maximum(top, 0.1 * NEGATIVE)
            total = sum(
                jnp.sum(jnp.exp2(a - (top - v)), axis=0, keepdims=True) for a, v in zip(tiles, bias)
            )
            if k == 0:
                span = slice(b * BLOCK, (b + 1) * BLOCK)
                both = jnp.maximum(top, own_top[:, span])
                total = total * jnp.exp2(top - both) + own_sum[:, span] * jnp.exp2(
                    own_top[:, span] - both
                )
                top = both
            for h in range(BLOCK // TOKENS):
                row = b * (BLOCK // TOKENS) + h
                span = slice(h * TOKENS, (h + 1) * TOKENS)
                out[who, row : row + 1, :] = top[:, span]
                out[who, 8 + row : 9 + row, :] = total[:, span]


def values_kernel(pos, info, qh, kh, kv, krh, vr, *refs):
    st = refs[:4]
    go = refs[4:8]
    dv, dvr, lt, out = refs[8:]
    y = pos[0]
    for k in range(4):
        who = responder(y, k)
        top = functools.reduce(jnp.maximum, [s[who, 0:8, :] for s in st])
        total = sum(s[who, 8:16, :] * jnp.exp2(s[who, 0:8, :] - top) for s in st)
        lt[k, :, :] = top + jnp.log2(total)
    dv[...] = jnp.zeros_like(dv)
    gb = heads_of(go[0], 0, HEADS)
    s = dot_nt(krh[...], qh[0]) * SCALE2
    p = jnp.where(causal(), jnp.exp2(s - joined(lt, 0, 0, HEADS)), 0.0).astype(BF16)
    own_dots = jnp.sum(p.astype(F32) * dot_nt(vr[...], gb), axis=0, keepdims=True)
    dvr[...] = dot_nn(p, gb)
    for k in range(4):
        who = responder(y, k)
        rows = pl.ds(pl.multiple_of(info[k, 0] * QUARTER, QUARTER), QUARTER)
        bias = biases_of(info, k, y)
        for b in range(QUERIES // BLOCK):
            per = BLOCK // TOKENS
            qb = qh[k, b * BLOCK : (b + 1) * BLOCK, :]
            gb = heads_of(go[k], b * per, per)
            row = joined(lt, k, b * per, per)
            scores = tiles_of(dot_nt(kh[rows, :], qb) * SCALE2)
            grads = tiles_of(dot_nt(kv[rows, HEAD:], gb))
            dots = own_dots[:, b * BLOCK : (b + 1) * BLOCK] if k == 0 else 0.0
            parts = []
            for a, g, v in zip(scores, grads, bias):
                p = jnp.exp2(a - (row - v)).astype(BF16)
                parts.append(p)
                dots = dots + jnp.sum(p.astype(F32) * g, axis=0, keepdims=True)
            dv[rows, :] += dot_nn(jnp.concatenate(parts, axis=0), gb)
            for h in range(per):
                out[who, b * per + h : b * per + h + 1, :] = dots[:, h * TOKENS : (h + 1) * TOKENS]


def grads_kernel(pos, info, lt, qh, kh, kv, krh, vr, kg, kr, *refs):
    dd = refs[:4]
    go = refs[4:8]
    q = refs[8:12]
    dq = refs[12:16]
    out, dkr, gains, kt, dk = refs[16:]
    y = pos[0]
    for p in range(2):
        kt[p, :, :] = kh[p * QUARTER : (p + 1) * QUARTER, :].T
    dk[...] = jnp.zeros_like(dk)
    gb = heads_of(go[0], 0, HEADS)
    dot_rows = []
    for k in range(4):
        who = responder(y, k)
        dots = sum(d[who] for d in dd)
        dot_rows.append(dots)
    s = dot_nt(krh[...], qh[0]) * SCALE2
    p = jnp.where(causal(), jnp.exp2(s - joined(lt, 0, 0, HEADS)), 0.0)
    every = jnp.concatenate([dot_rows[0][h : h + 1] for h in range(HEADS)], axis=1)
    ds = (p * (dot_nt(vr[...], gb) - every)).astype(BF16)
    own = dot_nn(ds, qh[0]) * SCALE
    own_dq = dot_nn(krh[...].T, ds)
    x = kr[...].astype(F32)
    dkr[...] = norm_back(x, kg[...], own)
    gain_k = jnp.sum(own * unit(x), axis=0, keepdims=True)
    gain_q = jnp.zeros((1, HEAD), F32)
    for k in (3, 1, 2, 0):
        who = responder(y, k)
        group = info[k, 0]
        rows = pl.ds(pl.multiple_of(group * QUARTER, QUARTER), QUARTER)
        bias = biases_of(info, k, y)
        for b in range(QUERIES // BLOCK):
            per = BLOCK // TOKENS
            qb = qh[k, b * BLOCK : (b + 1) * BLOCK, :]
            gb = heads_of(go[k], b * per, per)
            row = joined(lt, k, b * per, per)
            dots = jnp.concatenate(
                [dot_rows[k][b * per + h : b * per + h + 1] for h in range(per)], axis=1
            )
            scores = tiles_of(dot_nt(kh[rows, :], qb) * SCALE2)
            grads = tiles_of(dot_nt(kv[rows, HEAD:], gb))
            ds = jnp.concatenate(
                [
                    (jnp.exp2(a - (row - v)) * (g - dots)).astype(BF16)
                    for a, g, v in zip(scores, grads, bias)
                ],
                axis=0,
            )
            dk[rows, :] += dot_nn(ds, qb)
            total = dot_nn(kt[group], ds)
            if k == 0:
                total = total + own_dq[:, b * BLOCK : (b + 1) * BLOCK]
            total = total * SCALE
            for h in range(per):
                j = b * per + h
                part = total[:, h * TOKENS : (h + 1) * TOKENS].T
                dq[k][:, j * HEAD : (j + 1) * HEAD] = part
                u = unit(q[k][:, j * HEAD : (j + 1) * HEAD].astype(F32))
                gain_q = gain_q + jnp.sum(part * u, axis=0, keepdims=True)
    scaled = dk[...] * SCALE
    for c in range(Z):
        out[c, :ROWS, :] = scaled[c * ROWS : (c + 1) * ROWS].astype(BF16)
    u = unit(kv[:, :HEAD].astype(F32))
    gain_k = gain_k + jnp.sum(scaled * u, axis=0, keepdims=True)
    gains[...] = jnp.concatenate([gain_q, gain_k, jnp.zeros((6, HEAD), F32)], axis=0)


def terms_of(rest):
    terms = []
    for _ in range(3):
        terms.append(rest.astype(BF16))
        rest = rest - terms[-1].astype(F32)
    return terms


def pack_kernel(a, b, c, d, out):
    terms = terms_of(a[...] + b[...] + c[...] + d[...])
    out[...] = jnp.concatenate([*terms, jnp.zeros((8, HEAD), BF16)], axis=0)


def query_back_kernel(q, qg, mine, left, right, dks, out):
    for j in range(HEADS):
        span = slice(j * HEAD, (j + 1) * HEAD)
        dy = mine[:, span] + left[:, span] + right[:, span]
        dx = norm_back(q[:, span].astype(F32), qg[...], dy).astype(BF16)
        for h in range(X):
            out[h, :PART, span] = dx[h * PART : (h + 1) * PART]
    rows = sum(dks[s, ROWS:, :].astype(F32) for s in range(Z))
    terms = terms_of(rows[0:8] + rows[8:16] + rows[16:24])
    terms.append(jnp.zeros((8, QUERIES - 3 * HEAD), BF16))
    row = jnp.concatenate(terms, axis=1)
    row = jnp.concatenate([row, jnp.zeros_like(row)], axis=0)
    for h in range(X):
        out[h, PART:, :] = row


def key_back_kernel(k, kg, dks, dvs, dk, dv):
    dy = sum(dks[s, :ROWS, :].astype(F32) for s in range(Z))
    dk[...] = norm_back(k[...].astype(F32), kg[...], dy)
    dv[...] = sum(dvs[s] for s in range(Z))


def spread_kernel(parts, out, gains):
    total = jnp.zeros((8, HEAD), F32)
    for h in range(X):
        out[:, h * QUERIES : (h + 1) * QUERIES] = parts[h, :PART, :].astype(F32)
        rows = parts[h, PART:, :].astype(F32)[0:8]
        total = total + sum(rows[:, i * HEAD : (i + 1) * HEAD] for i in range(3))
    gains[...] = total


def call(kernel, out_shape, n_scalar, args, scratch=(), flops=0, nbytes=0, vmem=SMALL):
    specs = [pl.BlockSpec(memory_space=pltpu.SMEM)] * n_scalar
    specs += [pl.BlockSpec(memory_space=pltpu.VMEM)] * (len(args) - n_scalar)
    return pl.pallas_call(
        kernel,
        out_shape=out_shape,
        in_specs=specs,
        out_specs=jax.tree.map(lambda _: pl.BlockSpec(memory_space=pltpu.VMEM), out_shape),
        scratch_shapes=scratch,
        compiler_params=pltpu.CompilerParams(vmem_limit_bytes=vmem),
        cost_estimate=pl.CostEstimate(flops=flops, bytes_accessed=nbytes, transcendentals=0),
    )(*args)


def f32(*shape):
    return jax.ShapeDtypeStruct(shape, F32)


def bf16(*shape):
    return jax.ShapeDtypeStruct(shape, BF16)


def shift(x, axis, size, step):
    return lax.ppermute(x, axis, [(i, (i + step) % size) for i in range(size)])


def to_all(x, axis):
    return lax.all_to_all(x, axis, 0, 0, tiled=False)


def shards(
    prompt_key_input,
    prompt_value_input,
    resp_queries,
    response_key_input,
    response_value_input,
    q_gain,
    k_gain,
    groups,
    lengths,
    tiles,
    advantages,
    upstream,
):
    y = lax.axis_index("y")
    z = lax.axis_index("z")
    pos = jnp.stack([y, z]).astype(jnp.int32)
    qg = q_gain[None]
    kg = k_gain[None]
    k_raw = prompt_key_input[0]
    q_raw = resp_queries[0, 0]
    kr = response_key_input[0, 0]
    vr = response_value_input[0, 0]
    info = jnp.concatenate([groups[0], tiles[0, 0], jnp.zeros((79,), jnp.int32)])
    infos = [info] + [shift(info, "y", Y, k) for k in (-1, 1, 2)]

    q_before = shift(q_raw, "y", Y, 1)
    q_next = shift(q_raw, "y", Y, -1)
    q_far = shift(q_before, "y", Y, 1)
    tokens = jnp.arange(TOKENS, dtype=jnp.int32)[:, None]
    go = jnp.where(
        tokens < lengths[0, 0], -advantages[0, 0] * upstream[0, 0].astype(F32), 0.0
    ).astype(BF16)
    go_before = shift(go, "y", Y, 1)
    go_next = shift(go, "y", Y, -1)
    kv = jnp.concatenate([k_raw, prompt_value_input[0]], axis=1)
    kv = to_all(jnp.broadcast_to(kv[None], (Z, ROWS, 2 * HEAD)), "z").reshape(Z * ROWS, 2 * HEAD)
    kv, q_before, q_next, q_far, infos = lax.optimization_barrier(
        (kv, q_before, q_next, q_far, infos)
    )
    go_far = shift(go_next, "y", Y, -1)
    qs = (q_raw, q_next, q_before, q_far)
    gos = (go, go_next, go_before, go_far)
    info = jnp.stack(infos)

    unit_flops = 2 * 4 * QUERIES * QUARTER * HEAD
    qh, kh, krh, st = call(
        stats_kernel,
        (
            bf16(4, QUERIES, HEAD),
            bf16(2 * QUARTER, HEAD),
            bf16(TOKENS, HEAD),
            f32(Y, 16, 128),
        ),
        2,
        (pos, info, qg, kg, *qs, kv, kr),
        flops=2 * unit_flops,
        nbytes=1 << 22,
        vmem=VMEM,
    )
    sts = [st] + [shift(st, "y", Y, k) for k in (1, -1, 2)]
    dv, dvr, lt, dd = call(
        values_kernel,
        (
            f32(2 * QUARTER, HEAD),
            f32(TOKENS, HEAD),
            f32(4, HEADS, 128),
            f32(Y, HEADS, 128),
        ),
        2,
        (pos, info, qh, kh, kv, krh, vr, *sts, *gos),
        flops=4 * unit_flops,
        nbytes=1 << 22,
        vmem=VMEM,
    )
    dds = [dd] + [shift(dd, "y", Y, k) for k in (1, -1, 2)]
    dvs = to_all(dv.reshape(Z, ROWS, HEAD), "z")
    dq0, dq1, dq2, dq3, dk, dkr, gains = call(
        grads_kernel,
        (
            *[f32(TOKENS, QUERIES)] * 4,
            bf16(Z, ROWS + 32, HEAD),
            f32(TOKENS, HEAD),
            f32(8, HEAD),
        ),
        2,
        (pos, info, lt, qh, kh, kv, krh, vr, kg, kr, *dds, *gos, *qs),
        scratch=[pltpu.VMEM((2, HEAD, QUARTER), BF16), pltpu.VMEM((2 * QUARTER, HEAD), F32)],
        flops=5 * unit_flops,
        nbytes=1 << 22,
        vmem=VMEM,
    )

    half = QUERIES // 2
    far_up = shift(dq3[:, :half], "y", Y, 1)
    far_down = shift(dq3[:, half:], "y", Y, -1)
    to_next = jnp.concatenate([dq1[:, :half] + far_up, dq1[:, half:]], axis=1)
    to_before = jnp.concatenate([dq2[:, :half], dq2[:, half:] + far_down], axis=1)
    from_before = shift(to_next, "y", Y, 1)
    from_next = shift(to_before, "y", Y, -1)

    gains = gains + lax.ppermute(gains, "dp", [(0, 1), (1, 0)])
    gains = call(
        pack_kernel, bf16(32, HEAD), 0, [gains] + [shift(gains, "y", Y, k) for k in (1, -1, 2)]
    )
    dk = dk.at[:, ROWS:, :].set(jnp.broadcast_to(gains[None], (Z, 32, HEAD)))
    dk, dvs = lax.optimization_barrier((dk, dvs))
    dks = to_all(dk, "z")
    dq = call(
        query_back_kernel,
        bf16(X, PART + 16, QUERIES),
        0,
        (q_raw, qg, dq0, from_before, from_next, dks),
        nbytes=1 << 21,
    )
    dq = to_all(dq, "head")
    regrouped, gains = call(
        spread_kernel, (f32(PART, X * QUERIES), f32(8, HEAD)), 0, (dq,), nbytes=1 << 20
    )
    dk, dv = call(
        key_back_kernel,
        (f32(ROWS, HEAD), f32(ROWS, HEAD)),
        0,
        (k_raw, kg, dks, dvs),
        nbytes=1 << 20,
    )
    return (
        regrouped[None, None],
        dkr[None, None],
        dvr[None, None],
        dk[None],
        dv[None],
        gains[0],
        gains[1],
    )


def solution(mesh):
    sizes = mesh.devices.shape
    split = Mesh(mesh.devices.reshape(sizes[0], Z, Y, sizes[2]), ("dp", "z", "y", "head"))
    seq = ("z", "y")
    placed = (
        P("dp", seq, "head"),
        P("dp", seq, "head"),
        P("dp", seq, None, "head"),
        P("dp", seq, None, "head"),
        P("dp", seq, None, "head"),
        P(),
        P(),
        P("dp", seq),
        P("dp", seq),
        P("dp", seq, None),
        P("dp", seq),
        P("dp", seq, None, "head"),
    )
    return jax.shard_map(
        shards,
        mesh=split,
        in_specs=placed,
        out_specs=(
            P("dp", seq, "head", None),
            P("dp", seq, None, "head"),
            P("dp", seq, None, "head"),
            P("dp", seq, "head"),
            P("dp", seq, "head"),
            P(),
            P(),
        ),
        check_vma=False,
    )
```

```python
import functools

import jax
import jax.numpy as jnp
from jax import lax
from jax.experimental import pallas as pl
from jax.experimental.pallas import tpu as pltpu
from jax.sharding import Mesh
from jax.sharding import PartitionSpec as P

TILE = 64
HEAD = 128
HEADS = 8
TOKENS = 128
QUERIES = HEADS * TOKENS
ROWS = 192
Z = 8
Y = 4
X = 4
QUARTER = ROWS * Z // 2
BLOCK = 256
PART = TOKENS // X
PER_ROWS = ROWS // TILE
PER_PROMPT = PER_ROWS * Y
EPSILON = 1e-06
NEGATIVE = -1e30
SCALE = HEAD ** (-0.5)
SCALE2 = SCALE * 1.4426950408889634
VMEM = 56 * 1024 * 1024
SMALL = 12 * 1024 * 1024
F32 = jnp.float32
BF16 = jnp.bfloat16


def dot_nt(a, b):
    return lax.dot_general(a, b, (((1,), (1,)), ((), ())), preferred_element_type=F32)


def dot_nn(a, b):
    return jnp.dot(a, b, preferred_element_type=F32)


def dot_tn(a, b):
    return lax.dot_general(a, b, (((0,), (0,)), ((), ())), preferred_element_type=F32)


def unit(x):
    return x * lax.rsqrt(jnp.mean(x * x, axis=-1, keepdims=True) + EPSILON)


def norm_back(x, g, dy):
    r = lax.rsqrt(jnp.mean(x * x, axis=-1, keepdims=True) + EPSILON)
    u = x * r
    gy = g * dy
    return r * (gy - u * jnp.mean(u * gy, axis=-1, keepdims=True))


def responder(y, k):
    return lax.rem(y + (0, 1, 3, 2)[k], Y)


def heads_of(ref, first, count):
    return jnp.concatenate(
        [ref[:, j * HEAD : (j + 1) * HEAD] for j in range(first, first + count)], axis=0
    )


def tile_bias(info, who, y, t):
    index = 1 + (t // PER_ROWS) * PER_PROMPT + y * PER_ROWS + t % PER_ROWS
    return jnp.where(info[who, index] > 0, 0.0, NEGATIVE).astype(F32)


def causal():
    v = lax.broadcasted_iota(jnp.int32, (TOKENS, QUERIES), 0)
    t = lax.broadcasted_iota(jnp.int32, (TOKENS, QUERIES), 1) % TOKENS
    return v <= t


def joined(ref, k, first, count):
    return jnp.concatenate([ref[k, h : h + 1, :] for h in range(first, first + count)], axis=1)


def tiles_of(x):
    return [x[t * TILE : (t + 1) * TILE] for t in range(QUARTER // TILE)]


def biases_of(info, who, y):
    return [tile_bias(info, who, y, t) for t in range(QUARTER // TILE)]


def terms_of(rest):
    terms = []
    for _ in range(3):
        terms.append(rest.astype(BF16))
        rest = rest - terms[-1].astype(F32)
    return terms


def stats_kernel(pos, info, qg, kg, *refs):
    q = refs[:4]
    kv = refs[4]
    kr = refs[5]
    qh, kh, krh, out = refs[6:]
    y = pos[0]
    kh[...] = (unit(kv[:, :HEAD].astype(F32)) * kg[...]).astype(BF16)
    krh[...] = (unit(kr[...].astype(F32)) * kg[...]).astype(BF16)
    for k in range(4):
        for j in range(HEADS):
            u = unit(q[k][:TOKENS, j * HEAD : (j + 1) * HEAD].astype(F32))
            qh[k, j * TOKENS : (j + 1) * TOKENS, :] = (u * qg[...]).astype(BF16)
    own = jnp.where(causal(), dot_nt(krh[...], qh[0]) * SCALE2, NEGATIVE)
    own_top = jnp.max(own, axis=0, keepdims=True)
    own_sum = jnp.sum(jnp.exp2(own - own_top), axis=0, keepdims=True)
    for k in range(4):
        who = responder(y, k)
        first = pl.multiple_of(info[k, 0] * QUARTER, QUARTER)
        keys = kh[pl.ds(first, QUARTER), :]
        bias = biases_of(info, k, y)
        for b in range(QUERIES // BLOCK):
            qb = qh[k, b * BLOCK : (b + 1) * BLOCK, :]
            tiles = tiles_of(dot_nt(keys, qb) * SCALE2)
            top = functools.reduce(
                jnp.maximum,
                [jnp.max(a, axis=0, keepdims=True) + v for a, v in zip(tiles, bias)],
            )
            top = jnp.maximum(top, 0.1 * NEGATIVE)
            total = sum(
                jnp.sum(jnp.exp2(a - (top - v)), axis=0, keepdims=True) for a, v in zip(tiles, bias)
            )
            if k == 0:
                span = slice(b * BLOCK, (b + 1) * BLOCK)
                both = jnp.maximum(top, own_top[:, span])
                total = total * jnp.exp2(top - both) + own_sum[:, span] * jnp.exp2(
                    own_top[:, span] - both
                )
                top = both
            for h in range(BLOCK // TOKENS):
                row = b * (BLOCK // TOKENS) + h
                span = slice(h * TOKENS, (h + 1) * TOKENS)
                out[who, row : row + 1, :] = top[:, span]
                out[who, 8 + row : 9 + row, :] = total[:, span]


def values_kernel(pos, info, qh, kh, kv, krh, vr, *refs):
    st = refs[:4]
    go = refs[4:8]
    dv_out, dvr, lt, out, dv = refs[8:]
    y = pos[0]
    for k in range(4):
        who = responder(y, k)
        top = functools.reduce(jnp.maximum, [s[who, 0:8, :] for s in st])
        total = sum(s[who, 8:16, :] * jnp.exp2(s[who, 0:8, :] - top) for s in st)
        lt[k, :, :] = top + jnp.log2(total)
    dv[...] = jnp.zeros_like(dv)
    gb = heads_of(go[0], 0, HEADS)
    s = dot_nt(krh[...], qh[0]) * SCALE2
    p = jnp.where(causal(), jnp.exp2(s - joined(lt, 0, 0, HEADS)), 0.0).astype(BF16)
    own_dots = jnp.sum(p.astype(F32) * dot_nt(vr[...], gb), axis=0, keepdims=True)
    dvr[...] = dot_nn(p, gb)
    for k in range(4):
        who = responder(y, k)
        rows = pl.ds(pl.multiple_of(info[k, 0] * QUARTER, QUARTER), QUARTER)
        bias = biases_of(info, k, y)
        for b in range(QUERIES // BLOCK):
            per = BLOCK // TOKENS
            qb = qh[k, b * BLOCK : (b + 1) * BLOCK, :]
            gb = heads_of(go[k], b * per, per)
            row = joined(lt, k, b * per, per)
            scores = tiles_of(dot_nt(kh[rows, :], qb) * SCALE2)
            grads = tiles_of(dot_nt(kv[rows, HEAD:], gb))
            dots = own_dots[:, b * BLOCK : (b + 1) * BLOCK] if k == 0 else 0.0
            parts = []
            for a, g, v in zip(scores, grads, bias):
                p = jnp.exp2(a - (row - v)).astype(BF16)
                parts.append(p)
                dots = dots + jnp.sum(p.astype(F32) * g, axis=0, keepdims=True)
            dv[rows, :] += dot_nn(jnp.concatenate(parts, axis=0), gb)
            for h in range(per):
                out[who, b * per + h : b * per + h + 1, :] = dots[:, h * TOKENS : (h + 1) * TOKENS]
    dv_out[...] = dv[...].astype(BF16)


def grads_kernel(pos, info, lt, qh, kh, kv, krh, vr, kg, kr, dv, *refs):
    dd = refs[:4]
    go = refs[4:8]
    q = refs[8:12]
    dq = refs[12:15]
    far, out, dkr, kt, dk = refs[15:]
    y = pos[0]
    for p in range(2):
        kt[p, :, :] = kh[p * QUARTER : (p + 1) * QUARTER, :].T
    dk[...] = jnp.zeros_like(dk)
    gb = heads_of(go[0], 0, HEADS)
    dot_rows = []
    for k in range(4):
        who = responder(y, k)
        dots = sum(d[who] for d in dd)
        dot_rows.append(dots)
    s = dot_nt(krh[...], qh[0]) * SCALE2
    p = jnp.where(causal(), jnp.exp2(s - joined(lt, 0, 0, HEADS)), 0.0)
    every = jnp.concatenate([dot_rows[0][h : h + 1] for h in range(HEADS)], axis=1)
    ds = (p * (dot_nt(vr[...], gb) - every)).astype(BF16)
    own = dot_nn(ds, qh[0]) * SCALE
    own_dq = dot_nn(krh[...].T, ds)
    x = kr[...].astype(F32)
    dkr[...] = norm_back(x, kg[...], own)
    gain_k = jnp.sum(own * unit(x), axis=0, keepdims=True)
    gain_q = jnp.zeros((1, HEAD), F32)
    for k in (3, 1, 2, 0):
        who = responder(y, k)
        group = info[k, 0]
        rows = pl.ds(pl.multiple_of(group * QUARTER, QUARTER), QUARTER)
        bias = biases_of(info, k, y)
        for b in range(QUERIES // BLOCK):
            per = BLOCK // TOKENS
            qb = qh[k, b * BLOCK : (b + 1) * BLOCK, :]
            gb = heads_of(go[k], b * per, per)
            row = joined(lt, k, b * per, per)
            dots = jnp.concatenate(
                [dot_rows[k][b * per + h : b * per + h + 1] for h in range(per)], axis=1
            )
            scores = tiles_of(dot_nt(kh[rows, :], qb) * SCALE2)
            grads = tiles_of(dot_nt(kv[rows, HEAD:], gb))
            ds = jnp.concatenate(
                [
                    (jnp.exp2(a - (row - v)) * (g - dots)).astype(BF16)
                    for a, g, v in zip(scores, grads, bias)
                ],
                axis=0,
            )
            dk[rows, :] += dot_nn(ds, qb)
            total = dot_nn(kt[group], ds)
            if k == 0:
                total = total + own_dq[:, b * BLOCK : (b + 1) * BLOCK]
            total = total * SCALE
            for h in range(per):
                j = b * per + h
                part = total[:, h * TOKENS : (h + 1) * TOKENS].T
                if k == 3:
                    lane = j % (HEADS // 2) * HEAD
                    far[j // (HEADS // 2), :, lane : lane + HEAD] = part
                else:
                    dq[k][:, j * HEAD : (j + 1) * HEAD] = part
                u = unit(q[k][:TOKENS, j * HEAD : (j + 1) * HEAD].astype(F32))
                gain_q = gain_q + jnp.sum(part * u, axis=0, keepdims=True)
    scaled = dk[...] * SCALE
    for c in range(Z):
        span = slice(c * ROWS, (c + 1) * ROWS)
        out[c, :ROWS, :HEAD] = scaled[span].astype(BF16)
        out[c, :ROWS, HEAD:] = dv[span, :]
    u = unit(kv[:, :HEAD].astype(F32))
    gain_k = gain_k + jnp.sum(scaled * u, axis=0, keepdims=True)
    terms = terms_of(jnp.concatenate([gain_q, gain_k, jnp.zeros((6, HEAD), F32)], axis=0))
    rows = jnp.concatenate([*terms, jnp.zeros((8, HEAD), BF16)], axis=0)
    rows = jnp.concatenate([rows, jnp.zeros_like(rows)], axis=1)
    for c in range(Z):
        out[c, ROWS:, :] = rows


def query_back_kernel(q, qg, mine, left, right, gains, out):
    for j in range(HEADS):
        span = slice(j * HEAD, (j + 1) * HEAD)
        dy = mine[:, span] + left[:, span] + right[:, span]
        dx = norm_back(q[:, span].astype(F32), qg[...], dy).astype(BF16)
        for h in range(X):
            out[h, :PART, span] = dx[h * PART : (h + 1) * PART]
    terms = terms_of(sum(gains[i] for i in range(2 * Y)))
    terms.append(jnp.zeros((8, QUERIES - 3 * HEAD), BF16))
    row = jnp.concatenate(terms, axis=1)
    row = jnp.concatenate([row, jnp.zeros_like(row)], axis=0)
    for h in range(X):
        out[h, PART:, :] = row


def key_back_kernel(k, kg, parts, dk, dv):
    total = sum(parts[s, :ROWS, :].astype(F32) for s in range(Z))
    dk[...] = norm_back(k[...].astype(F32), kg[...], total[:, :HEAD])
    dv[...] = total[:, HEAD:]


def spread_kernel(parts, out, gains):
    total = jnp.zeros((8, HEAD), F32)
    for h in range(X):
        out[:, h * QUERIES : (h + 1) * QUERIES] = parts[h, :PART, :].astype(F32)
        rows = parts[h, PART:, :].astype(F32)[0:8]
        total = total + sum(rows[:, i * HEAD : (i + 1) * HEAD] for i in range(3))
    gains[...] = total


def call(kernel, out_shape, n_scalar, args, scratch=(), flops=0, nbytes=0, vmem=SMALL):
    specs = [pl.BlockSpec(memory_space=pltpu.SMEM)] * n_scalar
    specs += [pl.BlockSpec(memory_space=pltpu.VMEM)] * (len(args) - n_scalar)
    return pl.pallas_call(
        kernel,
        out_shape=out_shape,
        in_specs=specs,
        out_specs=jax.tree.map(lambda _: pl.BlockSpec(memory_space=pltpu.VMEM), out_shape),
        scratch_shapes=scratch,
        compiler_params=pltpu.CompilerParams(vmem_limit_bytes=vmem),
        cost_estimate=pl.CostEstimate(flops=flops, bytes_accessed=nbytes, transcendentals=0),
    )(*args)


def f32(*shape):
    return jax.ShapeDtypeStruct(shape, F32)


def bf16(*shape):
    return jax.ShapeDtypeStruct(shape, BF16)


def shift(x, axis, size, step):
    return lax.ppermute(x, axis, [(i, (i + step) % size) for i in range(size)])


def to_all(x, axis):
    return lax.all_to_all(x, axis, 0, 0, tiled=False)


def shards(
    prompt_key_input,
    prompt_value_input,
    resp_queries,
    response_key_input,
    response_value_input,
    q_gain,
    k_gain,
    groups,
    lengths,
    tiles,
    advantages,
    upstream,
):
    y = lax.axis_index("y")
    z = lax.axis_index("z")
    pos = jnp.stack([y, z]).astype(jnp.int32)
    qg = q_gain[None]
    kg = k_gain[None]
    k_raw = prompt_key_input[0]
    q_raw = resp_queries[0, 0]
    kr = response_key_input[0, 0]
    vr = response_value_input[0, 0]
    info = jnp.concatenate([groups[0], tiles[0, 0]]).astype(BF16)
    info = jnp.pad(info[None], ((0, 15), (0, QUERIES - 49)))
    q_ext = jnp.concatenate([q_raw, info], axis=0)

    q_before = shift(q_ext, "y", Y, 1)
    q_next = shift(q_ext, "y", Y, -1)
    q_far = shift(q_before, "y", Y, 1)
    tokens = jnp.arange(TOKENS, dtype=jnp.int32)[:, None]
    go = jnp.where(
        tokens < lengths[0, 0], -advantages[0, 0] * upstream[0, 0].astype(F32), 0.0
    ).astype(BF16)
    go_before = shift(go, "y", Y, 1)
    go_next = shift(go, "y", Y, -1)
    kv = jnp.concatenate([k_raw, prompt_value_input[0]], axis=1)
    kv = to_all(jnp.broadcast_to(kv[None], (Z, ROWS, 2 * HEAD)), "z").reshape(Z * ROWS, 2 * HEAD)
    kv, q_before, q_next, q_far = lax.optimization_barrier((kv, q_before, q_next, q_far))
    go_far = shift(go_next, "y", Y, -1)
    qs = (q_ext, q_next, q_before, q_far)
    gos = (go, go_next, go_before, go_far)
    info = jnp.stack([a[TOKENS, :128] for a in qs]).astype(jnp.int32)

    unit_flops = 2 * 4 * QUERIES * QUARTER * HEAD
    qh, kh, krh, st = call(
        stats_kernel,
        (
            bf16(4, QUERIES, HEAD),
            bf16(2 * QUARTER, HEAD),
            bf16(TOKENS, HEAD),
            f32(Y, 16, 128),
        ),
        2,
        (pos, info, qg, kg, *qs, kv, kr),
        flops=2 * unit_flops,
        nbytes=1 << 22,
        vmem=VMEM,
    )
    sts = [st] + [shift(st, "y", Y, k) for k in (1, -1, 2)]
    dv, dvr, lt, dd = call(
        values_kernel,
        (
            bf16(2 * QUARTER, HEAD),
            f32(TOKENS, HEAD),
            f32(4, HEADS, 128),
            f32(Y, HEADS, 128),
        ),
        2,
        (pos, info, qh, kh, kv, krh, vr, *sts, *gos),
        scratch=[pltpu.VMEM((2 * QUARTER, HEAD), F32)],
        flops=4 * unit_flops,
        nbytes=1 << 22,
        vmem=VMEM,
    )
    dds = [dd] + [shift(dd, "y", Y, k) for k in (1, -1, 2)]
    dq0, dq1, dq2, far, dkv, dkr = call(
        grads_kernel,
        (
            *[f32(TOKENS, QUERIES)] * 3,
            f32(2, TOKENS, QUERIES // 2),
            bf16(Z, ROWS + 32, 2 * HEAD),
            f32(TOKENS, HEAD),
        ),
        2,
        (pos, info, lt, qh, kh, kv, krh, vr, kg, kr, dv, *dds, *gos, *qs),
        scratch=[pltpu.VMEM((2, HEAD, QUARTER), BF16), pltpu.VMEM((2 * QUARTER, HEAD), F32)],
        flops=5 * unit_flops,
        nbytes=1 << 22,
        vmem=VMEM,
    )

    half = QUERIES // 2
    dkvs = to_all(dkv, "z")
    far_up = shift(far[0], "y", Y, 1)
    far_down = shift(far[1], "y", Y, -1)
    to_next = jnp.concatenate([dq1[:, :half] + far_up, dq1[:, half:]], axis=1)
    to_before = jnp.concatenate([dq2[:, :half], dq2[:, half:] + far_down], axis=1)
    from_before = shift(to_next, "y", Y, 1)
    from_next = shift(to_before, "y", Y, -1)
    gains = dkvs[:, ROWS : ROWS + 24, :HEAD].astype(F32).reshape(Z * 3, 8, HEAD).sum(axis=0)
    gains = to_all(jnp.broadcast_to(gains[None], (2 * Y, 8, HEAD)), ("dp", "y"))

    dq = call(
        query_back_kernel,
        bf16(X, PART + 16, QUERIES),
        0,
        (q_raw, qg, dq0, from_before, from_next, gains),
        nbytes=1 << 21,
    )
    dq = to_all(dq, "head")
    regrouped, gains = call(
        spread_kernel, (f32(PART, X * QUERIES), f32(8, HEAD)), 0, (dq,), nbytes=1 << 20
    )
    dk, dv = call(
        key_back_kernel,
        (f32(ROWS, HEAD), f32(ROWS, HEAD)),
        0,
        (k_raw, kg, dkvs),
        nbytes=1 << 20,
    )
    return (
        regrouped[None, None],
        dkr[None, None],
        dvr[None, None],
        dk[None],
        dv[None],
        gains[0],
        gains[1],
    )


def solution(mesh):
    sizes = mesh.devices.shape
    split = Mesh(mesh.devices.reshape(sizes[0], Z, Y, sizes[2]), ("dp", "z", "y", "head"))
    seq = ("z", "y")
    placed = (
        P("dp", seq, "head"),
        P("dp", seq, "head"),
        P("dp", seq, None, "head"),
        P("dp", seq, None, "head"),
        P("dp", seq, None, "head"),
        P(),
        P(),
        P("dp", seq),
        P("dp", seq),
        P("dp", seq, None),
        P("dp", seq),
        P("dp", seq, None, "head"),
    )
    return jax.shard_map(
        shards,
        mesh=split,
        in_specs=placed,
        out_specs=(
            P("dp", seq, "head", None),
            P("dp", seq, None, "head"),
            P("dp", seq, None, "head"),
            P("dp", seq, "head"),
            P("dp", seq, "head"),
            P(),
            P(),
        ),
        check_vma=False,
    )
```

```python
import functools

import jax
import jax.numpy as jnp
from jax import lax
from jax.experimental import pallas as pl
from jax.experimental.pallas import tpu as pltpu
from jax.sharding import Mesh
from jax.sharding import PartitionSpec as P

TILE = 64
HEAD = 128
HEADS = 8
TOKENS = 128
QUERIES = HEADS * TOKENS
ROWS = 192
Z = 8
Y = 4
X = 4
QUARTER = ROWS * Z // 2
BLOCK = 512
PART = TOKENS // X
PER_ROWS = ROWS // TILE
PER_PROMPT = PER_ROWS * Y
EPSILON = 1e-06
NEGATIVE = -1e30
SCALE = HEAD ** (-0.5)
SCALE2 = SCALE * 1.4426950408889634
VMEM = 56 * 1024 * 1024
SMALL = 12 * 1024 * 1024
F32 = jnp.float32
BF16 = jnp.bfloat16


def dot_nt(a, b):
    return lax.dot_general(a, b, (((1,), (1,)), ((), ())), preferred_element_type=F32)


def dot_nn(a, b):
    return jnp.dot(a, b, preferred_element_type=F32)


def dot_tn(a, b):
    return lax.dot_general(a, b, (((0,), (0,)), ((), ())), preferred_element_type=F32)


def unit(x):
    return x * lax.rsqrt(jnp.mean(x * x, axis=-1, keepdims=True) + EPSILON)


def norm_back(x, g, dy):
    r = lax.rsqrt(jnp.mean(x * x, axis=-1, keepdims=True) + EPSILON)
    u = x * r
    gy = g * dy
    return r * (gy - u * jnp.mean(u * gy, axis=-1, keepdims=True))


def responder(y, k):
    return lax.rem(y + (0, 1, 3, 2)[k], Y)


def heads_of(ref, first, count):
    return jnp.concatenate(
        [ref[:, j * HEAD : (j + 1) * HEAD] for j in range(first, first + count)], axis=0
    )


def tile_bias(info, who, y, t):
    index = 1 + (t // PER_ROWS) * PER_PROMPT + y * PER_ROWS + t % PER_ROWS
    return jnp.where(info[who, index] > 0, 0.0, NEGATIVE).astype(F32)


def causal():
    v = lax.broadcasted_iota(jnp.int32, (TOKENS, QUERIES), 0)
    t = lax.broadcasted_iota(jnp.int32, (TOKENS, QUERIES), 1) % TOKENS
    return v <= t


def joined(ref, k, first, count):
    return jnp.concatenate([ref[k, h : h + 1, :] for h in range(first, first + count)], axis=1)


def tiles_of(x):
    return [x[t * TILE : (t + 1) * TILE] for t in range(QUARTER // TILE)]


def biases_of(info, who, y):
    return [tile_bias(info, who, y, t) for t in range(QUARTER // TILE)]


def terms_of(rest):
    terms = []
    for _ in range(3):
        terms.append(rest.astype(BF16))
        rest = rest - terms[-1].astype(F32)
    return terms


def stats_kernel(pos, info, qg, kg, *refs):
    q = refs[:4]
    kv = refs[4]
    kr = refs[5]
    qh, kh, krh, out = refs[6:]
    y = pos[0]
    kh[...] = (unit(kv[:, :HEAD].astype(F32)) * kg[...]).astype(BF16)
    krh[...] = (unit(kr[...].astype(F32)) * kg[...]).astype(BF16)
    for k in range(4):
        for j in range(HEADS):
            u = unit(q[k][:TOKENS, j * HEAD : (j + 1) * HEAD].astype(F32))
            qh[k, j * TOKENS : (j + 1) * TOKENS, :] = (u * qg[...]).astype(BF16)
    own = jnp.where(causal(), dot_nt(krh[...], qh[0]) * SCALE2, NEGATIVE)
    own_top = jnp.max(own, axis=0, keepdims=True)
    own_sum = jnp.sum(jnp.exp2(own - own_top), axis=0, keepdims=True)
    for k in range(4):
        who = responder(y, k)
        first = pl.multiple_of(info[k, 0] * QUARTER, QUARTER)
        keys = kh[pl.ds(first, QUARTER), :]
        bias = biases_of(info, k, y)
        for b in range(QUERIES // BLOCK):
            qb = qh[k, b * BLOCK : (b + 1) * BLOCK, :]
            tiles = tiles_of(dot_nt(keys, qb) * SCALE2)
            top = functools.reduce(
                jnp.maximum,
                [jnp.max(a, axis=0, keepdims=True) + v for a, v in zip(tiles, bias)],
            )
            top = jnp.maximum(top, 0.1 * NEGATIVE)
            total = sum(
                jnp.sum(jnp.exp2(a - (top - v)), axis=0, keepdims=True) for a, v in zip(tiles, bias)
            )
            if k == 0:
                span = slice(b * BLOCK, (b + 1) * BLOCK)
                both = jnp.maximum(top, own_top[:, span])
                total = total * jnp.exp2(top - both) + own_sum[:, span] * jnp.exp2(
                    own_top[:, span] - both
                )
                top = both
            for h in range(BLOCK // TOKENS):
                row = b * (BLOCK // TOKENS) + h
                span = slice(h * TOKENS, (h + 1) * TOKENS)
                out[who, row : row + 1, :] = top[:, span]
                out[who, 8 + row : 9 + row, :] = total[:, span]


def values_kernel(pos, info, qh, kh, kv, krh, vr, *refs):
    st = refs[:4]
    go = refs[4:8]
    dv_out, dvr, lt, out, dv = refs[8:]
    y = pos[0]
    for k in range(4):
        who = responder(y, k)
        top = functools.reduce(jnp.maximum, [s[who, 0:8, :] for s in st])
        total = sum(s[who, 8:16, :] * jnp.exp2(s[who, 0:8, :] - top) for s in st)
        lt[k, :, :] = top + jnp.log2(total)
    dv[...] = jnp.zeros_like(dv)
    gb = heads_of(go[0], 0, HEADS)
    s = dot_nt(krh[...], qh[0]) * SCALE2
    p = jnp.where(causal(), jnp.exp2(s - joined(lt, 0, 0, HEADS)), 0.0).astype(BF16)
    own_dots = jnp.sum(p.astype(F32) * dot_nt(vr[...], gb), axis=0, keepdims=True)
    dvr[...] = dot_nn(p, gb)
    for k in range(4):
        who = responder(y, k)
        rows = pl.ds(pl.multiple_of(info[k, 0] * QUARTER, QUARTER), QUARTER)
        bias = biases_of(info, k, y)
        for b in range(QUERIES // BLOCK):
            per = BLOCK // TOKENS
            qb = qh[k, b * BLOCK : (b + 1) * BLOCK, :]
            gb = heads_of(go[k], b * per, per)
            row = joined(lt, k, b * per, per)
            scores = tiles_of(dot_nt(kh[rows, :], qb) * SCALE2)
            grads = tiles_of(dot_nt(kv[rows, HEAD:], gb))
            dots = own_dots[:, b * BLOCK : (b + 1) * BLOCK] if k == 0 else 0.0
            parts = []
            for a, g, v in zip(scores, grads, bias):
                p = jnp.exp2(a - (row - v)).astype(BF16)
                parts.append(p)
                dots = dots + jnp.sum(p.astype(F32) * g, axis=0, keepdims=True)
            dv[rows, :] += dot_nn(jnp.concatenate(parts, axis=0), gb)
            for h in range(per):
                out[who, b * per + h : b * per + h + 1, :] = dots[:, h * TOKENS : (h + 1) * TOKENS]
    dv_out[...] = dv[...].astype(BF16)


def grads_kernel(pos, info, lt, qh, kh, kv, krh, vr, kg, kr, dv, *refs):
    dd = refs[:4]
    go = refs[4:8]
    q = refs[8:12]
    dq = refs[12:15]
    far, out, dkr, kt, dk = refs[15:]
    y = pos[0]
    for p in range(2):
        kt[p, :, :] = kh[p * QUARTER : (p + 1) * QUARTER, :].T
    dk[...] = jnp.zeros_like(dk)
    gb = heads_of(go[0], 0, HEADS)
    dot_rows = []
    for k in range(4):
        who = responder(y, k)
        dots = sum(d[who] for d in dd)
        dot_rows.append(dots)
    s = dot_nt(krh[...], qh[0]) * SCALE2
    p = jnp.where(causal(), jnp.exp2(s - joined(lt, 0, 0, HEADS)), 0.0)
    every = jnp.concatenate([dot_rows[0][h : h + 1] for h in range(HEADS)], axis=1)
    ds = (p * (dot_nt(vr[...], gb) - every)).astype(BF16)
    own = dot_nn(ds, qh[0]) * SCALE
    own_dq = dot_nn(krh[...].T, ds)
    x = kr[...].astype(F32)
    dkr[...] = norm_back(x, kg[...], own)
    gain_k = jnp.sum(own * unit(x), axis=0, keepdims=True)
    gain_q = jnp.zeros((1, HEAD), F32)
    for k in (3, 1, 2, 0):
        who = responder(y, k)
        group = info[k, 0]
        rows = pl.ds(pl.multiple_of(group * QUARTER, QUARTER), QUARTER)
        bias = biases_of(info, k, y)
        for b in range(QUERIES // BLOCK):
            per = BLOCK // TOKENS
            qb = qh[k, b * BLOCK : (b + 1) * BLOCK, :]
            gb = heads_of(go[k], b * per, per)
            row = joined(lt, k, b * per, per)
            dots = jnp.concatenate(
                [dot_rows[k][b * per + h : b * per + h + 1] for h in range(per)], axis=1
            )
            scores = tiles_of(dot_nt(kh[rows, :], qb) * SCALE2)
            grads = tiles_of(dot_nt(kv[rows, HEAD:], gb))
            ds = jnp.concatenate(
                [
                    (jnp.exp2(a - (row - v)) * (g - dots)).astype(BF16)
                    for a, g, v in zip(scores, grads, bias)
                ],
                axis=0,
            )
            dk[rows, :] += dot_nn(ds, qb)
            total = dot_nn(kt[group], ds)
            if k == 0:
                total = total + own_dq[:, b * BLOCK : (b + 1) * BLOCK]
            total = total * SCALE
            for h in range(per):
                j = b * per + h
                part = total[:, h * TOKENS : (h + 1) * TOKENS].T
                if k == 3:
                    lane = j % (HEADS // 2) * HEAD
                    far[j // (HEADS // 2), :, lane : lane + HEAD] = part
                else:
                    dq[k][:, j * HEAD : (j + 1) * HEAD] = part
                u = unit(q[k][:TOKENS, j * HEAD : (j + 1) * HEAD].astype(F32))
                gain_q = gain_q + jnp.sum(part * u, axis=0, keepdims=True)
    scaled = dk[...] * SCALE
    for c in range(Z):
        span = slice(c * ROWS, (c + 1) * ROWS)
        out[c, :ROWS, :HEAD] = scaled[span].astype(BF16)
        out[c, :ROWS, HEAD:] = dv[span, :]
    u = unit(kv[:, :HEAD].astype(F32))
    gain_k = gain_k + jnp.sum(scaled * u, axis=0, keepdims=True)
    terms = terms_of(jnp.concatenate([gain_q, gain_k, jnp.zeros((6, HEAD), F32)], axis=0))
    terms.append(jnp.zeros((8, HEAD), BF16))
    rows = jnp.concatenate(
        [jnp.concatenate(terms[:2], axis=0), jnp.concatenate(terms[2:], axis=0)], axis=1
    )
    for c in range(Z):
        out[c, ROWS:, :] = rows


def query_back_kernel(pos, q, qg, mine, left, right, own, *refs):
    out, dx = refs[:3], refs[3]
    for j in range(HEADS):
        span = slice(j * HEAD, (j + 1) * HEAD)
        dy = mine[:, span] + left[:, span] + right[:, span]
        dx[:, span] = norm_back(q[:, span].astype(F32), qg[...], dy).astype(BF16)
    for k, ref in enumerate((own, *out)):
        part = lax.rem(pos[2] + k, X) * PART
        ref[...] = dx[pl.ds(pl.multiple_of(part, PART), PART), :]


def key_back_kernel(k, kg, parts, dk, dv):
    total = sum(parts[s, :ROWS, :].astype(F32) for s in range(Z))
    dk[...] = norm_back(k[...].astype(F32), kg[...], total[:, :HEAD])
    dv[...] = total[:, HEAD:]


def spread_kernel(pos, *refs):
    parts, out = refs[:4], refs[4]
    for k, ref in enumerate(parts):
        first = lax.rem(pos[2] + X - k, X) * QUERIES
        out[:, pl.ds(pl.multiple_of(first, QUERIES), QUERIES)] = ref[...].astype(F32)


def call(kernel, out_shape, n_scalar, args, scratch=(), flops=0, nbytes=0, vmem=SMALL):
    specs = [pl.BlockSpec(memory_space=pltpu.SMEM)] * n_scalar
    specs += [pl.BlockSpec(memory_space=pltpu.VMEM)] * (len(args) - n_scalar)
    return pl.pallas_call(
        kernel,
        out_shape=out_shape,
        in_specs=specs,
        out_specs=jax.tree.map(lambda _: pl.BlockSpec(memory_space=pltpu.VMEM), out_shape),
        scratch_shapes=scratch,
        compiler_params=pltpu.CompilerParams(vmem_limit_bytes=vmem),
        cost_estimate=pl.CostEstimate(flops=flops, bytes_accessed=nbytes, transcendentals=0),
    )(*args)


def f32(*shape):
    return jax.ShapeDtypeStruct(shape, F32)


def bf16(*shape):
    return jax.ShapeDtypeStruct(shape, BF16)


UNIT = 2 * 4 * QUERIES * QUARTER * HEAD


def run_stats(pos, info, qg, kg, qs, kv, kr):
    return call(
        stats_kernel,
        (
            bf16(4, QUERIES, HEAD),
            bf16(2 * QUARTER, HEAD),
            bf16(TOKENS, HEAD),
            f32(Y, 16, 128),
        ),
        2,
        (pos, info, qg, kg, *qs, kv, kr),
        flops=2 * UNIT,
        nbytes=1 << 22,
        vmem=VMEM,
    )


def run_values(pos, info, qh, kh, kv, krh, vr, sts, gos):
    return call(
        values_kernel,
        (
            bf16(2 * QUARTER, HEAD),
            f32(TOKENS, HEAD),
            f32(4, HEADS, 128),
            f32(Y, HEADS, 128),
        ),
        2,
        (pos, info, qh, kh, kv, krh, vr, *sts, *gos),
        scratch=[pltpu.VMEM((2 * QUARTER, HEAD), F32)],
        flops=4 * UNIT,
        nbytes=1 << 22,
        vmem=VMEM,
    )


def run_grads(pos, info, lt, qh, kh, kv, krh, vr, kg, kr, dv, dds, gos, qs):
    return call(
        grads_kernel,
        (
            *[f32(TOKENS, QUERIES)] * 3,
            f32(2, TOKENS, QUERIES // 2),
            bf16(Z, ROWS + 16, 2 * HEAD),
            f32(TOKENS, HEAD),
        ),
        2,
        (pos, info, lt, qh, kh, kv, krh, vr, kg, kr, dv, *dds, *gos, *qs),
        scratch=[pltpu.VMEM((2, HEAD, QUARTER), BF16), pltpu.VMEM((2 * QUARTER, HEAD), F32)],
        flops=5 * UNIT,
        nbytes=1 << 22,
        vmem=VMEM,
    )


def shift(x, axis, size, step):
    return lax.ppermute(x, axis, [(i, (i + step) % size) for i in range(size)])


def to_all(x, axis):
    return lax.all_to_all(x, axis, 0, 0, tiled=False)


def shards(
    prompt_key_input,
    prompt_value_input,
    resp_queries,
    response_key_input,
    response_value_input,
    q_gain,
    k_gain,
    groups,
    lengths,
    tiles,
    advantages,
    upstream,
):
    y = lax.axis_index("y")
    z = lax.axis_index("z")
    pos = jnp.stack([y, z, lax.axis_index("head")]).astype(jnp.int32)
    qg = q_gain[None]
    kg = k_gain[None]
    k_raw = prompt_key_input[0]
    q_raw = resp_queries[0, 0]
    kr = response_key_input[0, 0]
    vr = response_value_input[0, 0]
    info = jnp.concatenate([groups[0], tiles[0, 0]]).astype(BF16)
    info = jnp.pad(info[None], ((0, 15), (0, QUERIES - 49)))
    q_ext = jnp.concatenate([q_raw, info], axis=0)

    q_before = shift(q_ext, "y", Y, 1)
    q_next = shift(q_ext, "y", Y, -1)
    q_far = shift(q_before, "y", Y, 1)
    tokens = jnp.arange(TOKENS, dtype=jnp.int32)[:, None]
    go = jnp.where(
        tokens < lengths[0, 0], -advantages[0, 0] * upstream[0, 0].astype(F32), 0.0
    ).astype(BF16)
    go_before = shift(go, "y", Y, 1)
    go_next = shift(go, "y", Y, -1)
    kv = jnp.concatenate([k_raw, prompt_value_input[0]], axis=1)
    kv = to_all(jnp.broadcast_to(kv[None], (Z, ROWS, 2 * HEAD)), "z").reshape(Z * ROWS, 2 * HEAD)
    kv, q_before, q_next, q_far = lax.optimization_barrier((kv, q_before, q_next, q_far))
    go_far = shift(go_next, "y", Y, -1)
    qs = (q_ext, q_next, q_before, q_far)
    gos = (go, go_next, go_before, go_far)
    info = jnp.stack([a[TOKENS, :128] for a in qs]).astype(jnp.int32)

    qh, kh, krh, st = run_stats(pos, info, qg, kg, qs, kv, kr)
    sts = [st] + [shift(st, "y", Y, k) for k in (1, -1, 2)]
    dv, dvr, lt, dd = run_values(pos, info, qh, kh, kv, krh, vr, sts, gos)
    dds = [dd] + [shift(dd, "y", Y, k) for k in (1, -1, 2)]
    dq0, dq1, dq2, far, dkv, dkr = run_grads(
        pos, info, lt, qh, kh, kv, krh, vr, kg, kr, dv, dds, gos, qs
    )
    half = QUERIES // 2
    dkvs = to_all(dkv, "z")
    far_up = shift(far[0], "y", Y, 1)
    far_down = shift(far[1], "y", Y, -1)
    to_next = jnp.concatenate([dq1[:, :half] + far_up, dq1[:, half:]], axis=1)
    to_before = jnp.concatenate([dq2[:, :half], dq2[:, half:] + far_down], axis=1)
    from_before = shift(to_next, "y", Y, 1)
    from_next = shift(to_before, "y", Y, -1)
    rows = dkvs[:, ROWS:, :].astype(F32).sum(axis=0)
    gains = rows[0:8, :HEAD] + rows[8:16, :HEAD] + rows[0:8, HEAD:]
    gains = to_all(jnp.broadcast_to(gains[None], (2 * Y * X, 8, HEAD)), ("dp", "y", "head"))
    gains = gains.sum(axis=0)

    own, *parts = call(
        query_back_kernel,
        (bf16(PART, QUERIES),) * 4,
        1,
        (pos, q_raw, qg, dq0, from_before, from_next),
        scratch=[pltpu.VMEM((TOKENS, QUERIES), BF16)],
        nbytes=1 << 21,
    )
    parts = [own] + [shift(part, "head", X, k + 1) for k, part in enumerate(parts)]
    regrouped = call(
        spread_kernel, f32(PART, X * QUERIES), 1, (pos, *parts), nbytes=1 << 20
    )
    dk, dv = call(
        key_back_kernel,
        (f32(ROWS, HEAD), f32(ROWS, HEAD)),
        0,
        (k_raw, kg, dkvs),
        nbytes=1 << 20,
    )
    return (
        regrouped[None, None],
        dkr[None, None],
        dvr[None, None],
        dk[None],
        dv[None],
        gains[0],
        gains[1],
    )


def solution(mesh):
    sizes = mesh.devices.shape
    split = Mesh(mesh.devices.reshape(sizes[0], Z, Y, sizes[2]), ("dp", "z", "y", "head"))
    seq = ("z", "y")
    placed = (
        P("dp", seq, "head"),
        P("dp", seq, "head"),
        P("dp", seq, None, "head"),
        P("dp", seq, None, "head"),
        P("dp", seq, None, "head"),
        P(),
        P(),
        P("dp", seq),
        P("dp", seq),
        P("dp", seq, None),
        P("dp", seq),
        P("dp", seq, None, "head"),
    )
    return jax.shard_map(
        shards,
        mesh=split,
        in_specs=placed,
        out_specs=(
            P("dp", seq, "head", None),
            P("dp", seq, None, "head"),
            P("dp", seq, None, "head"),
            P("dp", seq, "head"),
            P("dp", seq, "head"),
            P(),
            P(),
        ),
        check_vma=False,
    )
```

```python
import functools

import jax
import jax.numpy as jnp
from jax import lax
from jax.experimental import pallas as pl
from jax.experimental.pallas import tpu as pltpu
from jax.sharding import Mesh
from jax.sharding import PartitionSpec as P

TILE = 64
HEAD = 128
HEADS = 8
TOKENS = 128
QUERIES = HEADS * TOKENS
ROWS = 192
Z = 8
Y = 4
X = 4
QUARTER = ROWS * Z // 2
BLOCK = 512
PART = TOKENS // X
PER_ROWS = ROWS // TILE
PER_PROMPT = PER_ROWS * Y
EPSILON = 1e-06
NEGATIVE = -1e30
SCALE = HEAD ** (-0.5)
SCALE2 = SCALE * 1.4426950408889634
VMEM = 50 * 1024 * 1024
SMALL = 12 * 1024 * 1024
F32 = jnp.float32
BF16 = jnp.bfloat16


def dot_nt(a, b):
    return lax.dot_general(a, b, (((1,), (1,)), ((), ())), preferred_element_type=F32)


def dot_nn(a, b):
    return jnp.dot(a, b, preferred_element_type=F32)


def dot_tn(a, b):
    return lax.dot_general(a, b, (((0,), (0,)), ((), ())), preferred_element_type=F32)


def unit(x):
    return x * lax.rsqrt(jnp.mean(x * x, axis=-1, keepdims=True) + EPSILON)


def norm_back(x, g, dy):
    r = lax.rsqrt(jnp.mean(x * x, axis=-1, keepdims=True) + EPSILON)
    u = x * r
    gy = g * dy
    return r * (gy - u * jnp.mean(u * gy, axis=-1, keepdims=True))


def responder(y, k):
    return lax.rem(y + (0, 1, 3, 2)[k], Y)


def heads_of(ref, first, count):
    return jnp.concatenate(
        [ref[:, j * HEAD : (j + 1) * HEAD] for j in range(first, first + count)], axis=0
    )


def tile_bias(info, who, y, t):
    index = 1 + (t // PER_ROWS) * PER_PROMPT + y * PER_ROWS + t % PER_ROWS
    return jnp.where(info[who, index] > 0, 0.0, NEGATIVE).astype(F32)


def causal():
    v = lax.broadcasted_iota(jnp.int32, (TOKENS, QUERIES), 0)
    t = lax.broadcasted_iota(jnp.int32, (TOKENS, QUERIES), 1) % TOKENS
    return v <= t


def joined(ref, k, first, count):
    return jnp.concatenate([ref[k, h : h + 1, :] for h in range(first, first + count)], axis=1)


def tiles_of(x):
    return [x[t * TILE : (t + 1) * TILE] for t in range(QUARTER // TILE)]


def biases_of(info, who, y):
    return [tile_bias(info, who, y, t) for t in range(QUARTER // TILE)]


def terms_of(rest):
    terms = []
    for _ in range(3):
        terms.append(rest.astype(BF16))
        rest = rest - terms[-1].astype(F32)
    return terms


def stats_kernel(pos, info, qg, kg, *refs):
    q = refs[:4]
    kv = refs[4]
    kr = refs[5]
    qh, kh, krh, out = refs[6:]
    y = pos[0]
    kh[...] = (unit(kv[:, :HEAD].astype(F32)) * kg[...]).astype(BF16)
    krh[...] = (unit(kr[...].astype(F32)) * kg[...]).astype(BF16)
    for k in range(4):
        for j in range(HEADS):
            u = unit(q[k][:TOKENS, j * HEAD : (j + 1) * HEAD].astype(F32))
            qh[k, j * TOKENS : (j + 1) * TOKENS, :] = (u * qg[...]).astype(BF16)
    own = jnp.where(causal(), dot_nt(krh[...], qh[0]) * SCALE2, NEGATIVE)
    own_top = jnp.max(own, axis=0, keepdims=True)
    own_sum = jnp.sum(jnp.exp2(own - own_top), axis=0, keepdims=True)
    for k in range(4):
        who = responder(y, k)
        first = pl.multiple_of(info[k, 0] * QUARTER, QUARTER)
        keys = kh[pl.ds(first, QUARTER), :]
        bias = biases_of(info, k, y)
        for b in range(QUERIES // BLOCK):
            qb = qh[k, b * BLOCK : (b + 1) * BLOCK, :]
            tiles = tiles_of(dot_nt(keys, qb) * SCALE2)
            top = functools.reduce(
                jnp.maximum,
                [jnp.max(a, axis=0, keepdims=True) + v for a, v in zip(tiles, bias)],
            )
            top = jnp.maximum(top, 0.1 * NEGATIVE)
            total = sum(
                jnp.sum(jnp.exp2(a - (top - v)), axis=0, keepdims=True) for a, v in zip(tiles, bias)
            )
            if k == 0:
                span = slice(b * BLOCK, (b + 1) * BLOCK)
                both = jnp.maximum(top, own_top[:, span])
                total = total * jnp.exp2(top - both) + own_sum[:, span] * jnp.exp2(
                    own_top[:, span] - both
                )
                top = both
            for h in range(BLOCK // TOKENS):
                row = b * (BLOCK // TOKENS) + h
                span = slice(h * TOKENS, (h + 1) * TOKENS)
                out[who, row : row + 1, :] = top[:, span]
                out[who, 8 + row : 9 + row, :] = total[:, span]


def values_kernel(pos, info, qh, kh, kv, krh, vr, *refs):
    st = refs[:4]
    go = refs[4:8]
    dv_out, dvr, lt, out, dv = refs[8:]
    y = pos[0]
    for k in range(4):
        who = responder(y, k)
        top = functools.reduce(jnp.maximum, [s[who, 0:8, :] for s in st])
        total = sum(s[who, 8:16, :] * jnp.exp2(s[who, 0:8, :] - top) for s in st)
        lt[k, :, :] = top + jnp.log2(total)
    dv[...] = jnp.zeros_like(dv)
    gb = heads_of(go[0], 0, HEADS)
    s = dot_nt(krh[...], qh[0]) * SCALE2
    p = jnp.where(causal(), jnp.exp2(s - joined(lt, 0, 0, HEADS)), 0.0).astype(BF16)
    own_dots = jnp.sum(p.astype(F32) * dot_nt(vr[...], gb), axis=0, keepdims=True)
    dvr[...] = dot_nn(p, gb)
    for k in range(4):
        who = responder(y, k)
        rows = pl.ds(pl.multiple_of(info[k, 0] * QUARTER, QUARTER), QUARTER)
        bias = biases_of(info, k, y)
        for b in range(QUERIES // BLOCK):
            per = BLOCK // TOKENS
            qb = qh[k, b * BLOCK : (b + 1) * BLOCK, :]
            gb = heads_of(go[k], b * per, per)
            row = joined(lt, k, b * per, per)
            scores = tiles_of(dot_nt(kh[rows, :], qb) * SCALE2)
            grads = tiles_of(dot_nt(kv[rows, HEAD:], gb))
            dots = own_dots[:, b * BLOCK : (b + 1) * BLOCK] if k == 0 else 0.0
            parts = []
            for a, g, v in zip(scores, grads, bias):
                p = jnp.exp2(a - (row - v)).astype(BF16)
                parts.append(p)
                dots = dots + jnp.sum(p.astype(F32) * g, axis=0, keepdims=True)
            dv[rows, :] += dot_nn(jnp.concatenate(parts, axis=0), gb)
            for h in range(per):
                out[who, b * per + h : b * per + h + 1, :] = dots[:, h * TOKENS : (h + 1) * TOKENS]
    dv_out[...] = dv[...].astype(BF16)


def grads_kernel(pos, info, lt, qh, kh, kv, krh, vr, kg, kr, dv, *refs):
    dd = refs[:4]
    go = refs[4:8]
    q = refs[8:12]
    dq = refs[12:15]
    far, out, dkr, kt, dk = refs[15:]
    y = pos[0]
    for p in range(2):
        kt[p, :, :] = kh[p * QUARTER : (p + 1) * QUARTER, :].T
    dk[...] = jnp.zeros_like(dk)
    gb = heads_of(go[0], 0, HEADS)
    dot_rows = []
    for k in range(4):
        who = responder(y, k)
        dots = sum(d[who] for d in dd)
        dot_rows.append(dots)
    s = dot_nt(krh[...], qh[0]) * SCALE2
    p = jnp.where(causal(), jnp.exp2(s - joined(lt, 0, 0, HEADS)), 0.0)
    every = jnp.concatenate([dot_rows[0][h : h + 1] for h in range(HEADS)], axis=1)
    ds = (p * (dot_nt(vr[...], gb) - every)).astype(BF16)
    own = dot_nn(ds, qh[0]) * SCALE
    own_dq = dot_nn(krh[...].T, ds)
    x = kr[...].astype(F32)
    dkr[...] = norm_back(x, kg[...], own)
    gain_k = jnp.sum(own * unit(x), axis=0, keepdims=True)
    gain_q = jnp.zeros((1, HEAD), F32)
    for k in (3, 1, 2, 0):
        who = responder(y, k)
        group = info[k, 0]
        rows = pl.ds(pl.multiple_of(group * QUARTER, QUARTER), QUARTER)
        bias = biases_of(info, k, y)
        for b in range(QUERIES // BLOCK):
            per = BLOCK // TOKENS
            qb = qh[k, b * BLOCK : (b + 1) * BLOCK, :]
            gb = heads_of(go[k], b * per, per)
            row = joined(lt, k, b * per, per)
            dots = jnp.concatenate(
                [dot_rows[k][b * per + h : b * per + h + 1] for h in range(per)], axis=1
            )
            scores = tiles_of(dot_nt(kh[rows, :], qb) * SCALE2)
            grads = tiles_of(dot_nt(kv[rows, HEAD:], gb))
            ds = jnp.concatenate(
                [
                    (jnp.exp2(a - (row - v)) * (g - dots)).astype(BF16)
                    for a, g, v in zip(scores, grads, bias)
                ],
                axis=0,
            )
            dk[rows, :] += dot_nn(ds, qb)
            total = dot_nn(kt[group], ds)
            if k == 0:
                total = total + own_dq[:, b * BLOCK : (b + 1) * BLOCK]
            total = total * SCALE
            for h in range(per):
                j = b * per + h
                part = total[:, h * TOKENS : (h + 1) * TOKENS].T
                if k == 3:
                    lane = j % (HEADS // 2) * HEAD
                    far[j // (HEADS // 2), :, lane : lane + HEAD] = part
                else:
                    dq[k][:, j * HEAD : (j + 1) * HEAD] = part
                u = unit(q[k][:TOKENS, j * HEAD : (j + 1) * HEAD].astype(F32))
                gain_q = gain_q + jnp.sum(part * u, axis=0, keepdims=True)
    scaled = dk[...] * SCALE
    for c in range(Z):
        span = slice(c * ROWS, (c + 1) * ROWS)
        out[c, :ROWS, :HEAD] = scaled[span].astype(BF16)
        out[c, :ROWS, HEAD:] = dv[span, :]
    u = unit(kv[:, :HEAD].astype(F32))
    gain_k = gain_k + jnp.sum(scaled * u, axis=0, keepdims=True)
    terms = terms_of(jnp.concatenate([gain_q, gain_k, jnp.zeros((6, HEAD), F32)], axis=0))
    terms.append(jnp.zeros((8, HEAD), BF16))
    rows = jnp.concatenate(
        [jnp.concatenate(terms[:2], axis=0), jnp.concatenate(terms[2:], axis=0)], axis=1
    )
    for c in range(Z):
        out[c, ROWS:, :] = rows


def query_back_kernel(pos, q, qg, mine, left, right, own, *refs):
    out, dx = refs[:3], refs[3]
    for j in range(HEADS):
        span = slice(j * HEAD, (j + 1) * HEAD)
        dy = mine[:, span] + left[:, span] + right[:, span]
        dx[:, span] = norm_back(q[:, span].astype(F32), qg[...], dy).astype(BF16)
    for k, ref in enumerate((own, *out)):
        part = lax.rem(pos[2] + k, X) * PART
        ref[...] = dx[pl.ds(pl.multiple_of(part, PART), PART), :]


def key_back_kernel(k, kg, parts, dk, dv):
    total = sum(parts[s, :ROWS, :].astype(F32) for s in range(Z))
    dk[...] = norm_back(k[...].astype(F32), kg[...], total[:, :HEAD])
    dv[...] = total[:, HEAD:]


def spread_kernel(pos, *refs):
    parts, out = refs[:4], refs[4]
    for k, ref in enumerate(parts):
        first = lax.rem(pos[2] + X - k, X) * QUERIES
        out[:, pl.ds(pl.multiple_of(first, QUERIES), QUERIES)] = ref[...].astype(F32)


def call(kernel, out_shape, n_scalar, args, scratch=(), flops=0, nbytes=0, vmem=SMALL):
    specs = [pl.BlockSpec(memory_space=pltpu.SMEM)] * n_scalar
    specs += [pl.BlockSpec(memory_space=pltpu.VMEM)] * (len(args) - n_scalar)
    return pl.pallas_call(
        kernel,
        out_shape=out_shape,
        in_specs=specs,
        out_specs=jax.tree.map(lambda _: pl.BlockSpec(memory_space=pltpu.VMEM), out_shape),
        scratch_shapes=scratch,
        compiler_params=pltpu.CompilerParams(vmem_limit_bytes=vmem),
        cost_estimate=pl.CostEstimate(flops=flops, bytes_accessed=nbytes, transcendentals=0),
    )(*args)


def f32(*shape):
    return jax.ShapeDtypeStruct(shape, F32)


def bf16(*shape):
    return jax.ShapeDtypeStruct(shape, BF16)


UNIT = 2 * 4 * QUERIES * QUARTER * HEAD


def run_stats(pos, info, qg, kg, qs, kv, kr):
    return call(
        stats_kernel,
        (
            bf16(4, QUERIES, HEAD),
            bf16(2 * QUARTER, HEAD),
            bf16(TOKENS, HEAD),
            f32(Y, 16, 128),
        ),
        2,
        (pos, info, qg, kg, *qs, kv, kr),
        flops=2 * UNIT,
        nbytes=1 << 22,
        vmem=VMEM,
    )


def run_values(pos, info, qh, kh, kv, krh, vr, sts, gos):
    return call(
        values_kernel,
        (
            bf16(2 * QUARTER, HEAD),
            f32(TOKENS, HEAD),
            f32(4, HEADS, 128),
            f32(Y, HEADS, 128),
        ),
        2,
        (pos, info, qh, kh, kv, krh, vr, *sts, *gos),
        scratch=[pltpu.VMEM((2 * QUARTER, HEAD), F32)],
        flops=4 * UNIT,
        nbytes=1 << 22,
        vmem=VMEM,
    )


def run_grads(pos, info, lt, qh, kh, kv, krh, vr, kg, kr, dv, dds, gos, qs):
    return call(
        grads_kernel,
        (
            *[f32(TOKENS, QUERIES)] * 3,
            f32(2, TOKENS, QUERIES // 2),
            bf16(Z, ROWS + 16, 2 * HEAD),
            f32(TOKENS, HEAD),
        ),
        2,
        (pos, info, lt, qh, kh, kv, krh, vr, kg, kr, dv, *dds, *gos, *qs),
        scratch=[pltpu.VMEM((2, HEAD, QUARTER), BF16), pltpu.VMEM((2 * QUARTER, HEAD), F32)],
        flops=5 * UNIT,
        nbytes=1 << 22,
        vmem=VMEM,
    )


def shift(x, axis, size, step):
    return lax.ppermute(x, axis, [(i, (i + step) % size) for i in range(size)])


def to_all(x, axis):
    return lax.all_to_all(x, axis, 0, 0, tiled=False)


def shards(
    prompt_key_input,
    prompt_value_input,
    resp_queries,
    response_key_input,
    response_value_input,
    q_gain,
    k_gain,
    groups,
    lengths,
    tiles,
    advantages,
    upstream,
):
    y = lax.axis_index("y")
    z = lax.axis_index("z")
    pos = jnp.stack([y, z, lax.axis_index("head")]).astype(jnp.int32)
    qg = q_gain[None]
    kg = k_gain[None]
    k_raw = prompt_key_input[0]
    q_raw = resp_queries[0, 0]
    kr = response_key_input[0, 0]
    vr = response_value_input[0, 0]
    info = jnp.concatenate([groups[0], tiles[0, 0]]).astype(BF16)
    info = jnp.pad(info[None], ((0, 15), (0, QUERIES - 49)))
    q_ext = jnp.concatenate([q_raw, info], axis=0)

    q_before = shift(q_ext, "y", Y, 1)
    q_next = shift(q_ext, "y", Y, -1)
    q_far = shift(q_before, "y", Y, 1)
    tokens = jnp.arange(TOKENS, dtype=jnp.int32)[:, None]
    go = jnp.where(
        tokens < lengths[0, 0], -advantages[0, 0] * upstream[0, 0].astype(F32), 0.0
    ).astype(BF16)
    go_before = shift(go, "y", Y, 1)
    go_next = shift(go, "y", Y, -1)
    kv = jnp.concatenate([k_raw, prompt_value_input[0]], axis=1)
    kv = to_all(jnp.broadcast_to(kv[None], (Z, ROWS, 2 * HEAD)), "z").reshape(Z * ROWS, 2 * HEAD)
    kv, q_before, q_next, q_far = lax.optimization_barrier((kv, q_before, q_next, q_far))
    go_far = shift(go_next, "y", Y, -1)
    qs = (q_ext, q_next, q_before, q_far)
    gos = (go, go_next, go_before, go_far)
    info = jnp.stack([a[TOKENS, :128] for a in qs]).astype(jnp.int32)

    qh, kh, krh, st = run_stats(pos, info, qg, kg, qs, kv, kr)
    sts = [st] + [shift(st, "y", Y, k) for k in (1, -1, 2)]
    dv, dvr, lt, dd = run_values(pos, info, qh, kh, kv, krh, vr, sts, gos)
    dds = [dd] + [shift(dd, "y", Y, k) for k in (1, -1, 2)]
    dq0, dq1, dq2, far, dkv, dkr = run_grads(
        pos, info, lt, qh, kh, kv, krh, vr, kg, kr, dv, dds, gos, qs
    )
    half = QUERIES // 2
    dkvs = to_all(dkv, "z")
    far_up = shift(far[0], "y", Y, 1)
    far_down = shift(far[1], "y", Y, -1)
    to_next = jnp.concatenate([dq1[:, :half] + far_up, dq1[:, half:]], axis=1)
    to_before = jnp.concatenate([dq2[:, :half], dq2[:, half:] + far_down], axis=1)
    from_before = shift(to_next, "y", Y, 1)
    from_next = shift(to_before, "y", Y, -1)
    rows = dkvs[:, ROWS:, :].astype(F32).sum(axis=0)
    gains = rows[0:8, :HEAD] + rows[8:16, :HEAD] + rows[0:8, HEAD:]
    gains = to_all(jnp.broadcast_to(gains[None], (2 * Y * X, 8, HEAD)), ("dp", "y", "head"))
    gains = gains.sum(axis=0)

    own, *parts = call(
        query_back_kernel,
        (bf16(PART, QUERIES),) * 4,
        1,
        (pos, q_raw, qg, dq0, from_before, from_next),
        scratch=[pltpu.VMEM((TOKENS, QUERIES), BF16)],
        nbytes=1 << 21,
    )
    parts = [own] + [shift(part, "head", X, k + 1) for k, part in enumerate(parts)]
    regrouped = call(
        spread_kernel, f32(PART, X * QUERIES), 1, (pos, *parts), nbytes=1 << 20
    )
    dk, dv = call(
        key_back_kernel,
        (f32(ROWS, HEAD), f32(ROWS, HEAD)),
        0,
        (k_raw, kg, dkvs),
        nbytes=1 << 20,
    )
    return (
        regrouped[None, None],
        dkr[None, None],
        dvr[None, None],
        dk[None],
        dv[None],
        gains[0],
        gains[1],
    )


def solution(mesh):
    sizes = mesh.devices.shape
    split = Mesh(mesh.devices.reshape(sizes[0], Z, Y, sizes[2]), ("dp", "z", "y", "head"))
    seq = ("z", "y")
    placed = (
        P("dp", seq, "head"),
        P("dp", seq, "head"),
        P("dp", seq, None, "head"),
        P("dp", seq, None, "head"),
        P("dp", seq, None, "head"),
        P(),
        P(),
        P("dp", seq),
        P("dp", seq),
        P("dp", seq, None),
        P("dp", seq),
        P("dp", seq, None, "head"),
    )
    return jax.shard_map(
        shards,
        mesh=split,
        in_specs=placed,
        out_specs=(
            P("dp", seq, "head", None),
            P("dp", seq, None, "head"),
            P("dp", seq, None, "head"),
            P("dp", seq, "head"),
            P("dp", seq, "head"),
            P(),
            P(),
        ),
        check_vma=False,
    )
```

```python
import functools

import jax
import jax.numpy as jnp
from jax import lax
from jax.experimental import pallas as pl
from jax.experimental.pallas import tpu as pltpu
from jax.sharding import Mesh
from jax.sharding import PartitionSpec as P

TILE = 64
HEAD = 128
HEADS = 8
TOKENS = 128
QUERIES = HEADS * TOKENS
ROWS = 192
Z = 8
Y = 4
X = 4
QUARTER = ROWS * Z // 2
BLOCK = 512
PART = TOKENS // X
PER_ROWS = ROWS // TILE
PER_PROMPT = PER_ROWS * Y
EPSILON = 1e-06
NEGATIVE = -1e30
SCALE = HEAD ** (-0.5)
SCALE2 = SCALE * 1.4426950408889634
VMEM = 50 * 1024 * 1024
SMALL = 12 * 1024 * 1024
F32 = jnp.float32
BF16 = jnp.bfloat16


def dot_nt(a, b):
    return lax.dot_general(a, b, (((1,), (1,)), ((), ())), preferred_element_type=F32)


def dot_nn(a, b):
    return jnp.dot(a, b, preferred_element_type=F32)


def dot_tn(a, b):
    return lax.dot_general(a, b, (((0,), (0,)), ((), ())), preferred_element_type=F32)


def unit(x):
    return x * lax.rsqrt(jnp.mean(x * x, axis=-1, keepdims=True) + EPSILON)


def norm_back(x, g, dy):
    r = lax.rsqrt(jnp.mean(x * x, axis=-1, keepdims=True) + EPSILON)
    u = x * r
    gy = g * dy
    return r * (gy - u * jnp.mean(u * gy, axis=-1, keepdims=True))


def responder(y, k):
    return lax.rem(y + (0, 1, 3, 2)[k], Y)


def heads_of(ref, first, count):
    return jnp.concatenate(
        [ref[:, j * HEAD : (j + 1) * HEAD] for j in range(first, first + count)], axis=0
    )


def tile_bias(info, who, y, t):
    index = 1 + (t // PER_ROWS) * PER_PROMPT + y * PER_ROWS + t % PER_ROWS
    return jnp.where(info[who, index] > 0, 0.0, NEGATIVE).astype(F32)


def causal():
    v = lax.broadcasted_iota(jnp.int32, (TOKENS, QUERIES), 0)
    t = lax.broadcasted_iota(jnp.int32, (TOKENS, QUERIES), 1) % TOKENS
    return v <= t


def joined(ref, k, first, count):
    return jnp.concatenate([ref[k, h : h + 1, :] for h in range(first, first + count)], axis=1)


def tiles_of(x):
    return [x[t * TILE : (t + 1) * TILE] for t in range(QUARTER // TILE)]


def biases_of(info, who, y):
    return [tile_bias(info, who, y, t) for t in range(QUARTER // TILE)]


def terms_of(rest):
    terms = []
    for _ in range(3):
        terms.append(rest.astype(BF16).astype(F32))
        rest = rest - terms[-1]
    return terms


def stats_kernel(pos, info, qg, kg, *refs):
    q = refs[:4]
    kv = refs[4]
    kr = refs[5]
    qh, kh, krh, out = refs[6:]
    y = pos[0]
    kh[...] = (unit(kv[:, :HEAD].astype(F32)) * kg[...]).astype(BF16)
    krh[...] = (unit(kr[...].astype(F32)) * kg[...]).astype(BF16)
    for k in range(4):
        for j in range(HEADS):
            u = unit(q[k][:TOKENS, j * HEAD : (j + 1) * HEAD].astype(F32))
            qh[k, j * TOKENS : (j + 1) * TOKENS, :] = (u * qg[...]).astype(BF16)
    own = jnp.where(causal(), dot_nt(krh[...], qh[0]) * SCALE2, NEGATIVE)
    own_top = jnp.max(own, axis=0, keepdims=True)
    own_sum = jnp.sum(jnp.exp2(own - own_top), axis=0, keepdims=True)
    for k in range(4):
        who = responder(y, k)
        first = pl.multiple_of(info[k, 0] * QUARTER, QUARTER)
        keys = kh[pl.ds(first, QUARTER), :]
        bias = biases_of(info, k, y)
        for b in range(QUERIES // BLOCK):
            qb = qh[k, b * BLOCK : (b + 1) * BLOCK, :]
            tiles = tiles_of(dot_nt(keys, qb) * SCALE2)
            top = functools.reduce(
                jnp.maximum,
                [jnp.max(a, axis=0, keepdims=True) + v for a, v in zip(tiles, bias)],
            )
            top = jnp.maximum(top, 0.1 * NEGATIVE)
            total = sum(
                jnp.sum(jnp.exp2(a - (top - v)), axis=0, keepdims=True) for a, v in zip(tiles, bias)
            )
            if k == 0:
                span = slice(b * BLOCK, (b + 1) * BLOCK)
                both = jnp.maximum(top, own_top[:, span])
                total = total * jnp.exp2(top - both) + own_sum[:, span] * jnp.exp2(
                    own_top[:, span] - both
                )
                top = both
            for h in range(BLOCK // TOKENS):
                row = b * (BLOCK // TOKENS) + h
                span = slice(h * TOKENS, (h + 1) * TOKENS)
                out[who, row : row + 1, :] = top[:, span]
                out[who, 8 + row : 9 + row, :] = total[:, span]


def values_kernel(pos, info, qh, kh, kv, krh, vr, *refs):
    st = refs[:4]
    go = refs[4:8]
    dv_out, dvr, lt, out, dv = refs[8:]
    y = pos[0]
    for k in range(4):
        who = responder(y, k)
        top = functools.reduce(jnp.maximum, [s[who, 0:8, :] for s in st])
        total = sum(s[who, 8:16, :] * jnp.exp2(s[who, 0:8, :] - top) for s in st)
        lt[k, :, :] = top + jnp.log2(total)
    dv[...] = jnp.zeros_like(dv)
    gb = heads_of(go[0], 0, HEADS)
    s = dot_nt(krh[...], qh[0]) * SCALE2
    p = jnp.where(causal(), jnp.exp2(s - joined(lt, 0, 0, HEADS)), 0.0).astype(BF16)
    own_dots = jnp.sum(p.astype(F32) * dot_nt(vr[...], gb), axis=0, keepdims=True)
    dvr[...] = dot_nn(p, gb)
    for k in range(4):
        who = responder(y, k)
        rows = pl.ds(pl.multiple_of(info[k, 0] * QUARTER, QUARTER), QUARTER)
        bias = biases_of(info, k, y)
        for b in range(QUERIES // BLOCK):
            per = BLOCK // TOKENS
            qb = qh[k, b * BLOCK : (b + 1) * BLOCK, :]
            gb = heads_of(go[k], b * per, per)
            row = joined(lt, k, b * per, per)
            scores = tiles_of(dot_nt(kh[rows, :], qb) * SCALE2)
            grads = tiles_of(dot_nt(kv[rows, HEAD:], gb))
            dots = own_dots[:, b * BLOCK : (b + 1) * BLOCK] if k == 0 else 0.0
            parts = []
            for a, g, v in zip(scores, grads, bias):
                p = jnp.exp2(a - (row - v)).astype(BF16)
                parts.append(p)
                dots = dots + jnp.sum(p.astype(F32) * g, axis=0, keepdims=True)
            dv[rows, :] += dot_nn(jnp.concatenate(parts, axis=0), gb)
            for h in range(per):
                out[who, b * per + h : b * per + h + 1, :] = dots[:, h * TOKENS : (h + 1) * TOKENS]
    dv_out[...] = dv[...].astype(BF16)


def grads_kernel(pos, info, lt, qh, kh, kv, krh, vr, kg, kr, dv, *refs):
    dd = refs[:4]
    go = refs[4:8]
    q = refs[8:12]
    dq = refs[12:15]
    far, out, dkr, kt, dk = refs[15:]
    y = pos[0]
    for p in range(2):
        kt[p, :, :] = kh[p * QUARTER : (p + 1) * QUARTER, :].T
    dk[...] = jnp.zeros_like(dk)
    gb = heads_of(go[0], 0, HEADS)
    dot_rows = []
    for k in range(4):
        who = responder(y, k)
        dots = sum(d[who] for d in dd)
        dot_rows.append(dots)
    s = dot_nt(krh[...], qh[0]) * SCALE2
    p = jnp.where(causal(), jnp.exp2(s - joined(lt, 0, 0, HEADS)), 0.0)
    every = jnp.concatenate([dot_rows[0][h : h + 1] for h in range(HEADS)], axis=1)
    ds = (p * (dot_nt(vr[...], gb) - every)).astype(BF16)
    own = dot_nn(ds, qh[0]) * SCALE
    own_dq = dot_nn(krh[...].T, ds)
    x = kr[...].astype(F32)
    dkr[...] = norm_back(x, kg[...], own)
    gain_k = jnp.sum(own * unit(x), axis=0, keepdims=True)
    gain_q = jnp.zeros((1, HEAD), F32)
    for k in (3, 1, 2, 0):
        who = responder(y, k)
        group = info[k, 0]
        rows = pl.ds(pl.multiple_of(group * QUARTER, QUARTER), QUARTER)
        bias = biases_of(info, k, y)
        for b in range(QUERIES // BLOCK):
            per = BLOCK // TOKENS
            qb = qh[k, b * BLOCK : (b + 1) * BLOCK, :]
            gb = heads_of(go[k], b * per, per)
            row = joined(lt, k, b * per, per)
            dots = jnp.concatenate(
                [dot_rows[k][b * per + h : b * per + h + 1] for h in range(per)], axis=1
            )
            scores = tiles_of(dot_nt(kh[rows, :], qb) * SCALE2)
            grads = tiles_of(dot_nt(kv[rows, HEAD:], gb))
            ds = jnp.concatenate(
                [
                    (jnp.exp2(a - (row - v)) * (g - dots)).astype(BF16)
                    for a, g, v in zip(scores, grads, bias)
                ],
                axis=0,
            )
            dk[rows, :] += dot_nn(ds, qb)
            total = dot_nn(kt[group], ds)
            if k == 0:
                total = total + own_dq[:, b * BLOCK : (b + 1) * BLOCK]
            total = total * SCALE
            for h in range(per):
                j = b * per + h
                part = total[:, h * TOKENS : (h + 1) * TOKENS].T
                if k == 3:
                    lane = j % (HEADS // 2) * HEAD
                    far[j // (HEADS // 2), :, lane : lane + HEAD] = part
                else:
                    dq[k][:, j * HEAD : (j + 1) * HEAD] = part
                u = unit(q[k][:TOKENS, j * HEAD : (j + 1) * HEAD].astype(F32))
                gain_q = gain_q + jnp.sum(part * u, axis=0, keepdims=True)
    scaled = dk[...] * SCALE
    for c in range(Z):
        span = slice(c * ROWS, (c + 1) * ROWS)
        out[c, :ROWS, :HEAD] = scaled[span].astype(BF16)
        out[c, :ROWS, HEAD:] = dv[span, :]
    u = unit(kv[:, :HEAD].astype(F32))
    gain_k = gain_k + jnp.sum(scaled * u, axis=0, keepdims=True)
    terms = terms_of(jnp.concatenate([gain_q, gain_k, jnp.zeros((6, HEAD), F32)], axis=0))
    terms.append(jnp.zeros((8, HEAD), F32))
    rows = jnp.concatenate(
        [jnp.concatenate(terms[:2], axis=0), jnp.concatenate(terms[2:], axis=0)], axis=1
    ).astype(BF16)
    for c in range(Z):
        out[c, ROWS:, :] = rows


def query_back_kernel(pos, q, qg, mine, left, right, own, *refs):
    out, dx = refs[:3], refs[3]
    for j in range(HEADS):
        span = slice(j * HEAD, (j + 1) * HEAD)
        dy = mine[:, span] + left[:, span] + right[:, span]
        dx[:, span] = norm_back(q[:, span].astype(F32), qg[...], dy).astype(BF16)
    for k, ref in enumerate((own, *out)):
        part = lax.rem(pos[2] + k, X) * PART
        ref[...] = dx[pl.ds(pl.multiple_of(part, PART), PART), :]


def key_back_kernel(k, kg, parts, dk, dv):
    total = sum(parts[s, :ROWS, :].astype(F32) for s in range(Z))
    dk[...] = norm_back(k[...].astype(F32), kg[...], total[:, :HEAD])
    dv[...] = total[:, HEAD:]


def spread_kernel(pos, *refs):
    parts, out = refs[:4], refs[4]
    for k, ref in enumerate(parts):
        first = lax.rem(pos[2] + X - k, X) * QUERIES
        out[:, pl.ds(pl.multiple_of(first, QUERIES), QUERIES)] = ref[...].astype(F32)


def call(kernel, out_shape, n_scalar, args, scratch=(), flops=0, nbytes=0, vmem=SMALL):
    specs = [pl.BlockSpec(memory_space=pltpu.SMEM)] * n_scalar
    specs += [pl.BlockSpec(memory_space=pltpu.VMEM)] * (len(args) - n_scalar)
    return pl.pallas_call(
        kernel,
        out_shape=out_shape,
        in_specs=specs,
        out_specs=jax.tree.map(lambda _: pl.BlockSpec(memory_space=pltpu.VMEM), out_shape),
        scratch_shapes=scratch,
        compiler_params=pltpu.CompilerParams(vmem_limit_bytes=vmem),
        cost_estimate=pl.CostEstimate(flops=flops, bytes_accessed=nbytes, transcendentals=0),
    )(*args)


def f32(*shape):
    return jax.ShapeDtypeStruct(shape, F32)


def bf16(*shape):
    return jax.ShapeDtypeStruct(shape, BF16)


UNIT = 2 * 4 * QUERIES * QUARTER * HEAD


def run_stats(pos, info, qg, kg, qs, kv, kr):
    return call(
        stats_kernel,
        (
            bf16(4, QUERIES, HEAD),
            bf16(2 * QUARTER, HEAD),
            bf16(TOKENS, HEAD),
            f32(Y, 16, 128),
        ),
        2,
        (pos, info, qg, kg, *qs, kv, kr),
        flops=2 * UNIT,
        nbytes=1 << 22,
        vmem=VMEM,
    )


def run_values(pos, info, qh, kh, kv, krh, vr, sts, gos):
    return call(
        values_kernel,
        (
            bf16(2 * QUARTER, HEAD),
            f32(TOKENS, HEAD),
            f32(4, HEADS, 128),
            f32(Y, HEADS, 128),
        ),
        2,
        (pos, info, qh, kh, kv, krh, vr, *sts, *gos),
        scratch=[pltpu.VMEM((2 * QUARTER, HEAD), F32)],
        flops=4 * UNIT,
        nbytes=1 << 22,
        vmem=VMEM,
    )


def run_grads(pos, info, lt, qh, kh, kv, krh, vr, kg, kr, dv, dds, gos, qs):
    return call(
        grads_kernel,
        (
            *[f32(TOKENS, QUERIES)] * 3,
            f32(2, TOKENS, QUERIES // 2),
            bf16(Z, ROWS + 16, 2 * HEAD),
            f32(TOKENS, HEAD),
        ),
        2,
        (pos, info, lt, qh, kh, kv, krh, vr, kg, kr, dv, *dds, *gos, *qs),
        scratch=[pltpu.VMEM((2, HEAD, QUARTER), BF16), pltpu.VMEM((2 * QUARTER, HEAD), F32)],
        flops=5 * UNIT,
        nbytes=1 << 22,
        vmem=VMEM,
    )


def shift(x, axis, size, step):
    return lax.ppermute(x, axis, [(i, (i + step) % size) for i in range(size)])


def to_all(x, axis):
    return lax.all_to_all(x, axis, 0, 0, tiled=False)


def shards(
    prompt_key_input,
    prompt_value_input,
    resp_queries,
    response_key_input,
    response_value_input,
    q_gain,
    k_gain,
    groups,
    lengths,
    tiles,
    advantages,
    upstream,
):
    y = lax.axis_index("y")
    z = lax.axis_index("z")
    pos = jnp.stack([y, z, lax.axis_index("head")]).astype(jnp.int32)
    qg = q_gain[None]
    kg = k_gain[None]
    k_raw = prompt_key_input[0]
    q_raw = resp_queries[0, 0]
    kr = response_key_input[0, 0]
    vr = response_value_input[0, 0]
    info = jnp.concatenate([groups[0], tiles[0, 0]]).astype(BF16)
    info = jnp.pad(info[None], ((0, 15), (0, QUERIES - 49)))
    q_ext = jnp.concatenate([q_raw, info], axis=0)

    q_before = shift(q_ext, "y", Y, 1)
    q_next = shift(q_ext, "y", Y, -1)
    q_far = shift(q_before, "y", Y, 1)
    tokens = jnp.arange(TOKENS, dtype=jnp.int32)[:, None]
    go = jnp.where(
        tokens < lengths[0, 0], -advantages[0, 0] * upstream[0, 0].astype(F32), 0.0
    ).astype(BF16)
    go_before = shift(go, "y", Y, 1)
    go_next = shift(go, "y", Y, -1)
    kv = jnp.concatenate([k_raw, prompt_value_input[0]], axis=1)
    kv = to_all(jnp.broadcast_to(kv[None], (Z, ROWS, 2 * HEAD)), "z").reshape(Z * ROWS, 2 * HEAD)
    kv, q_before, q_next, q_far = lax.optimization_barrier((kv, q_before, q_next, q_far))
    go_far = shift(go_next, "y", Y, -1)
    qs = (q_ext, q_next, q_before, q_far)
    gos = (go, go_next, go_before, go_far)
    info = jnp.stack([a[TOKENS, :128] for a in qs]).astype(jnp.int32)

    qh, kh, krh, st = run_stats(pos, info, qg, kg, qs, kv, kr)
    sts = [st] + [shift(st, "y", Y, k) for k in (1, -1, 2)]
    dv, dvr, lt, dd = run_values(pos, info, qh, kh, kv, krh, vr, sts, gos)
    dds = [dd] + [shift(dd, "y", Y, k) for k in (1, -1, 2)]
    dq0, dq1, dq2, far, dkv, dkr = run_grads(
        pos, info, lt, qh, kh, kv, krh, vr, kg, kr, dv, dds, gos, qs
    )
    half = QUERIES // 2
    dkvs = to_all(dkv, "z")
    far_up = shift(far[0], "y", Y, 1)
    far_down = shift(far[1], "y", Y, -1)
    to_next = jnp.concatenate([dq1[:, :half] + far_up, dq1[:, half:]], axis=1)
    to_before = jnp.concatenate([dq2[:, :half], dq2[:, half:] + far_down], axis=1)
    from_before = shift(to_next, "y", Y, 1)
    from_next = shift(to_before, "y", Y, -1)
    rows = dkvs[:, ROWS:, :].astype(F32).sum(axis=0)
    gains = rows[0:8, :HEAD] + rows[8:16, :HEAD] + rows[0:8, HEAD:]
    gains = to_all(jnp.broadcast_to(gains[None], (2 * Y * X, 8, HEAD)), ("dp", "y", "head"))
    gains = gains.sum(axis=0)

    own, *parts = call(
        query_back_kernel,
        (bf16(PART, QUERIES),) * 4,
        1,
        (pos, q_raw, qg, dq0, from_before, from_next),
        scratch=[pltpu.VMEM((TOKENS, QUERIES), BF16)],
        nbytes=1 << 21,
    )
    parts = [own] + [shift(part, "head", X, k + 1) for k, part in enumerate(parts)]
    regrouped = call(
        spread_kernel, f32(PART, X * QUERIES), 1, (pos, *parts), nbytes=1 << 20
    )
    dk, dv = call(
        key_back_kernel,
        (f32(ROWS, HEAD), f32(ROWS, HEAD)),
        0,
        (k_raw, kg, dkvs),
        nbytes=1 << 20,
    )
    return (
        regrouped[None, None],
        dkr[None, None],
        dvr[None, None],
        dk[None],
        dv[None],
        gains[0],
        gains[1],
    )


def solution(mesh):
    sizes = mesh.devices.shape
    split = Mesh(mesh.devices.reshape(sizes[0], Z, Y, sizes[2]), ("dp", "z", "y", "head"))
    seq = ("z", "y")
    placed = (
        P("dp", seq, "head"),
        P("dp", seq, "head"),
        P("dp", seq, None, "head"),
        P("dp", seq, None, "head"),
        P("dp", seq, None, "head"),
        P(),
        P(),
        P("dp", seq),
        P("dp", seq),
        P("dp", seq, None),
        P("dp", seq),
        P("dp", seq, None, "head"),
    )
    return jax.shard_map(
        shards,
        mesh=split,
        in_specs=placed,
        out_specs=(
            P("dp", seq, "head", None),
            P("dp", seq, None, "head"),
            P("dp", seq, None, "head"),
            P("dp", seq, "head"),
            P("dp", seq, "head"),
            P(),
            P(),
        ),
        check_vma=False,
    )
```
